128 devices in a mesh: seq: 8 (over y_lo, x), tile: 16 (over z, y_hi, core).
Axes of the slice: x: 4, y: 4 (y_hi: 2, y_lo: 2; y = y_hi * 2 + y_lo), z: 4, core: 2. Of those that a mesh axis runs over, the one named last changes fastest.
Arguments:
- transformer_latents: bfloat16 [16, 64, 1024], P('seq', 'tile'), may hold values from -6 to 6
- tile_arrangement: int32 [8, 32], P('seq'), may hold values from 0 to 31, each once within a row
- entry_conv_weight: bfloat16 [3, 3, 3, 16, 384], replicated, may hold values from -0.3125 to 0.3125
- first_norm_gain: float32 [384], replicated, may hold values from 0.1 to 1.9
- first_conv_weight: bfloat16 [3, 3, 3, 384, 384], replicated, may hold values from -0.0625 to 0.0625
- second_norm_gain: float32 [384], replicated, may hold values from 0.1 to 1.9
- second_conv_weight: bfloat16 [3, 3, 3, 384, 384], replicated, may hold values from -0.0625 to 0.0625
- temporal_upscale_weight: bfloat16 [3, 384, 768], replicated, may hold values from -0.1875 to 0.1875
- spatial_upscale_weight: bfloat16 [3, 3, 384, 192], replicated, may hold values from -0.109375 to 0.109375
Outputs:
- decoded: bfloat16 [32, 128, 128, 192], P('seq', 'tile')
The draws below stay inside these ranges and needn't reach their ends.
Inputs may be any that keep to these rules, and one draw needn't show every extreme that they name: Each row of tile_arrangement lists every number from 0 to 31 exactly once.
All inputs are finite; a program needn't handle non-finite values.
Results may differ from the reference program's by a relative error of at most 0.02.
Values may be sent and summed in bfloat16 or wider, within the bound.
A program may use at most 192 MiB of HBM per device.

```python
import jax
import jax.numpy as jnp
from jax import lax

LATENT_CHANNELS = 16
C = 384
CO = 192
BLOCK_FRAMES = 2
STRIP_ROWS = 4
LATENT_COLUMNS = 64
REQS = 4
FRAMES = 4
TOTAL_FRAMES = 16
LATENT_ROWS = 64
N_SEQ = 8
N_TILE = 16


def levels(rng, extent, shards, least, largest):
    level, own = 1.0, jax.random.fold_in(rng, 6)
    for dim, shards_of in shards:
        draws = jnp.exp(jax.random.uniform(jax.random.fold_in(own, dim), (shards_of,), jnp.float32, least / len(shards), largest / len(shards)))
        level = level * jnp.repeat(draws, extent[dim] // shards_of).reshape([-1 if axis == dim else 1 for axis in range(len(extent))])
    return level


def scatter_about(own_key, extent, spread, limit, pieces=(), dtype=jnp.bfloat16):
    level = levels(own_key, extent, pieces, -0.22, 0.18) if pieces else 1.0
    values = jax.random.normal(own_key, extent, jnp.float32) * spread * level
    return jnp.minimum(jnp.maximum(values, -limit), limit).astype(dtype)


def setup_inputs(seed: int = 0) -> dict:
    streams_of = jax.random.split(jax.random.key(seed), 10)
    return {
        "transformer_latents": scatter_about(streams_of[0], (TOTAL_FRAMES, LATENT_ROWS, LATENT_COLUMNS * LATENT_CHANNELS), 1.0, 6.0, ((0, 8), (1, 16))),
        "tile_arrangement": jax.vmap(lambda own: jax.random.permutation(own, BLOCK_FRAMES * N_TILE))(jax.random.split(streams_of[1], N_SEQ)).reshape((N_SEQ, BLOCK_FRAMES * N_TILE)).astype(jnp.int32),
        "entry_conv_weight": scatter_about(streams_of[2], (3, 3, 3, LATENT_CHANNELS, C), (27 * LATENT_CHANNELS) ** -0.5, 0.3125),
        "first_norm_gain": jnp.clip(1.0 + 0.18 * jax.random.normal(streams_of[3], (C,), jnp.float32), 0.1, 1.9),
        "first_conv_weight": scatter_about(streams_of[4], (3, 3, 3, C, C), (27 * C) ** -0.5, 0.0625),
        "second_norm_gain": jnp.clip(1.0 + 0.18 * jax.random.normal(streams_of[5], (C,), jnp.float32), 0.1, 1.9),
        "second_conv_weight": scatter_about(streams_of[6], (3, 3, 3, C, C), (27 * C) ** -0.5, 0.0625),
        "temporal_upscale_weight": scatter_about(streams_of[7], (3, C, 2 * C), (3 * C) ** -0.5, 0.1875),
        "spatial_upscale_weight": scatter_about(streams_of[8], (3, 3, C, CO), (9 * C) ** -0.5, 0.109375),
    }


epsilon = 1e-06

def causal_conv(values, weight):
    padded = jnp.pad(values.astype(jnp.float32), ((2, 0), (1, 1), (1, 1), (0, 0)))
    return lax.conv_general_dilated(padded[None], weight.astype(jnp.float32), (1, 1, 1), 'VALID', dimension_numbers=('NDHWC', 'DHWIO', 'NDHWC'), precision=lax.Precision.HIGHEST)[0]

def normed_silu(values, gain):
    widened = values.astype(jnp.float32)
    mean_square = lax.optimization_barrier(jnp.mean(widened * widened, axis=-1, keepdims=True))
    return jax.nn.silu(widened * lax.rsqrt(mean_square + epsilon) * gain)

def decode_clip(video_segment, entry_conv_weight, first_norm_gain, first_conv_weight, second_norm_gain, second_conv_weight, temporal_upscale_weight, spatial_upscale_weight):
    first = causal_conv(video_segment, entry_conv_weight).astype(jnp.bfloat16)
    hidden_one = normed_silu(first, first_norm_gain).astype(jnp.bfloat16)
    middle = causal_conv(hidden_one, first_conv_weight)
    hidden_two = normed_silu(middle, second_norm_gain).astype(jnp.bfloat16)
    second = (first.astype(jnp.float32) + causal_conv(hidden_two, second_conv_weight)).astype(jnp.bfloat16)
    padded = jnp.pad(second.astype(jnp.float32), ((2, 0), (0, 0), (0, 0), (0, 0)))
    frames = second.shape[0]
    summed = jnp.zeros(second.shape[:3] + (2 * C,), jnp.float32)
    for tap_time in range(3):
        summed = summed + jnp.einsum('thwc,cd->thwd', padded[tap_time:tap_time + frames], temporal_upscale_weight[tap_time].astype(jnp.float32), precision=lax.Precision.HIGHEST)
    split = summed.reshape(frames, LATENT_ROWS, LATENT_COLUMNS, 2, C)
    doubled = jnp.transpose(split, (0, 3, 1, 2, 4)).reshape(2 * frames, LATENT_ROWS, LATENT_COLUMNS, C).astype(jnp.bfloat16)
    larger = jnp.repeat(jnp.repeat(doubled, 2, axis=1), 2, axis=2).astype(jnp.float32)
    decoded = lax.conv_general_dilated(larger, spatial_upscale_weight.astype(jnp.float32), (1, 1), ((1, 1), (1, 1)), dimension_numbers=('NHWC', 'HWIO', 'NHWC'), precision=lax.Precision.HIGHEST)
    return decoded.astype(jnp.bfloat16)

def reference(transformer_latents, tile_arrangement, entry_conv_weight, first_norm_gain, first_conv_weight, second_norm_gain, second_conv_weight, temporal_upscale_weight, spatial_upscale_weight):
    segment_parts = transformer_latents.reshape(N_SEQ, BLOCK_FRAMES, N_TILE, STRIP_ROWS, LATENT_COLUMNS * LATENT_CHANNELS)
    segment_parts = jnp.transpose(segment_parts, (0, 2, 1, 3, 4)).reshape(N_SEQ, N_TILE * BLOCK_FRAMES, STRIP_ROWS, LATENT_COLUMNS * LATENT_CHANNELS)
    inverse = jnp.argsort(tile_arrangement, axis=1).astype(jnp.int32)
    placed = jnp.take_along_axis(segment_parts, inverse[:, :, None, None], axis=1)
    latents = placed.reshape(N_SEQ * BLOCK_FRAMES, N_TILE * STRIP_ROWS, LATENT_COLUMNS, LATENT_CHANNELS)
    clips = latents.reshape(REQS, FRAMES, LATENT_ROWS, LATENT_COLUMNS, LATENT_CHANNELS)

    def decode_one(video_segment):
        return decode_clip(video_segment, entry_conv_weight, first_norm_gain, first_conv_weight, second_norm_gain, second_conv_weight, temporal_upscale_weight, spatial_upscale_weight)
    decoded = lax.map(decode_one, clips)
    return decoded.reshape(2 * TOTAL_FRAMES, 2 * LATENT_ROWS, 2 * LATENT_COLUMNS, CO)
```

```python
import functools

import jax
import jax.numpy as jnp
from jax import lax
from jax.experimental import pallas as pl
from jax.experimental.pallas import tpu as pltpu
from jax.sharding import PartitionSpec as P

EPS = 1e-06
MESH = pl.DeviceIdType.MESH
F32 = jnp.float32
BF16 = jnp.bfloat16

FRAMES = 4
BLOCK = 2
ROWS = 4
COLS = 64
LAT = 16
C = 384
CO = 192
BANDS = 16
TALL = ROWS + 2
CELLS = ROWS * COLS


def silu_norm(v, gain):
    mean = jnp.sum(v * v, axis=-1, keepdims=True) * (1.0 / C)
    u = v * lax.rsqrt(mean + EPS) * gain
    return u / (1.0 + jnp.exp(-u))


def column(shape):
    return lax.broadcasted_iota(jnp.int32, shape, 0)


def shifted(h):
    col = column(h.shape)
    left = jnp.where(col == 0, 0.0, pltpu.roll(h, 1, 0))
    right = jnp.where(col == COLS - 1, 0.0, pltpu.roll(h, COLS - 1, 0))
    return left, right


def put_row(ref, t, y, h):
    left, right = shifted(h)
    ref[t, y, :, 0:C] = left.astype(BF16)
    ref[t, y, :, C : 2 * C] = h.astype(BF16)
    ref[t, y, :, 2 * C : 3 * C] = right.astype(BF16)


def stem_kernel(
    lat_ref,
    arr_ref,
    we_hbm,
    g1_ref,
    w1_hbm,
    g2_ref,
    w2_hbm,
    wt_hbm,
    out_ref,
    gath,
    lat4,
    late,
    lhs,
    rlo,
    rhi,
    patch,
    mid,
    first,
    h1,
    h2,
    acc,
    s_ref,
    we,
    w1,
    w2,
    wt,
    wsem,
    gsend,
    grecv,
    psem,
    hsend,
    hrecv,
    ssend,
    srecv,
):
    seq = lax.axis_index("seq")
    band = lax.axis_index("tile")
    half = lax.rem(seq, 2)
    mate = seq + 1 - 2 * half

    loads = []
    for p in range(9):
        loads.append(
            pltpu.make_async_copy(
                we_hbm.at[pl.ds(48 * p, 48)], we.at[pl.ds(64 * p, 48)], wsem.at[p]
            )
        )
    for k in range(3):
        loads.append(
            pltpu.make_async_copy(w1_hbm.at[2 - k], w1.at[:, pl.ds(k * C, C)], wsem.at[9 + k])
        )
    for k in range(3):
        loads.append(
            pltpu.make_async_copy(w2_hbm.at[2 - k], w2.at[:, pl.ds(k * C, C)], wsem.at[12 + k])
        )
    loads.append(pltpu.make_async_copy(wt_hbm, wt, wsem.at[15]))

    barrier = pltpu.get_barrier_semaphore()
    for d in range(1, BANDS):
        pl.semaphore_signal(
            barrier, inc=1, device_id=(seq, lax.rem(band + d, BANDS)), device_id_type=MESH
        )
    pl.semaphore_signal(barrier, inc=1, device_id=(mate, band), device_id_type=MESH)
    for load in loads:
        load.start()
    pl.semaphore_wait(barrier, BANDS)

    pushes = []
    for d in range(1, BANDS):
        pushes.append(
            pltpu.make_async_remote_copy(
                src_ref=lat_ref,
                dst_ref=gath.at[pl.ds(2 * band, 2)],
                send_sem=gsend.at[d],
                recv_sem=grecv.at[d],
                device_id=(seq, lax.rem(band + d, BANDS)),
                device_id_type=MESH,
            )
        )
    for push in pushes:
        push.start()
    gath[pl.ds(2 * band, 2)] = lat_ref[...]

    for p in range(9):
        we[pl.ds(64 * p + 48, 16)] = jnp.zeros((16, C), BF16)
    we[pl.ds(576, 64)] = jnp.zeros((64, C), BF16)
    rlo[0:2] = jnp.zeros((2, 8, COLS, 128), BF16)
    rhi[0:2] = jnp.zeros((2, 8, COLS, 128), BF16)
    s_ref[0:2] = jnp.zeros((2, TALL, COLS, C), BF16)
    spots = []
    for i in range(BLOCK):
        for o in (-1, 0, 1):
            target = i * BANDS + band + o
            spot = jnp.int32(0)
            for n in range(2 * BANDS):
                spot = jnp.where(arr_ref[0, n] == target, n, spot)
            spots.append(spot)

    for push in pushes:
        push.wait_recv()

    has_up = (band > 0).astype(F32)
    has_down = (band < BANDS - 1).astype(F32)
    picked = []
    for i in range(BLOCK):
        above = gath[spots[3 * i]].astype(F32) * has_up
        own = gath[spots[3 * i + 1]].astype(F32)
        below = gath[spots[3 * i + 2]].astype(F32) * has_down
        picked.append(jnp.concatenate([above[2:4], own, below[0:2]], axis=0))
    lat4[half] = jnp.concatenate(picked, axis=0).astype(BF16)
    swap = pltpu.make_async_remote_copy(
        src_ref=lat4.at[half],
        dst_ref=lat4.at[half],
        send_sem=psem.at[0],
        recv_sem=psem.at[1],
        device_id=(mate, band),
        device_id_type=MESH,
    )
    swap.start()
    swap.wait_recv()

    lat = lat4[...].reshape(4 * 8, COLS * LAT).astype(F32)
    lane = lax.broadcasted_iota(jnp.int32, lat.shape, 1)
    late[0] = jnp.where(lane < LAT, 0.0, pltpu.roll(lat, LAT, 1))
    late[1] = lat
    late[2] = jnp.where(lane >= (COLS - 1) * LAT, 0.0, pltpu.roll(lat, (COLS - 1) * LAT, 1))
    spread = (
        lax.rem(lax.broadcasted_iota(jnp.int32, (16, COLS * LAT), 1), 256) // LAT
        == lax.broadcasted_iota(jnp.int32, (16, COLS * LAT), 0)
    ).astype(F32)

    @pl.loop(0, 4 * 8)
    def _(r):
        for e in range(3):
            row = late[e, pl.ds(r, 1), :]
            full = (jnp.broadcast_to(row, (16, COLS * LAT)) * spread).astype(BF16)
            for g in range(4):
                lhs[r, pl.ds(16 * g, 16), 256 * e : 256 * (e + 1)] = full[
                    :, 256 * g : 256 * (g + 1)
                ]

    kk = lax.broadcasted_iota(jnp.int32, (768, 256), 0)
    nn = lax.broadcasted_iota(jnp.int32, (768, 256), 1)
    inside = lax.rem(nn, 128)
    want = jnp.where(
        nn < 128, inside, inside - 64
    )
    place = ((want >= 0) & (want < 48) & (want // LAT == kk // 256) & (lax.rem(want, LAT) == lax.rem(kk, LAT)))
    place = place.astype(F32).astype(BF16)

    @pl.loop(0, 4)
    def _(t):
        r = jnp.dot(
            lhs[pl.ds(8 * t, 8)].reshape(8 * COLS, 768), place, preferred_element_type=F32
        ).astype(BF16)
        rlo[t + 2] = r[:, 0:128].reshape(8, COLS, 128)
        rhi[t + 2] = r[:, 128:256].reshape(8, COLS, 128)

    for load in loads[:9]:
        load.wait()

    @pl.loop(0, 4)
    def _(t):
        taps = [(a, b) for a in range(3) for b in range(3)]
        for q in range(5):
            a, b = taps[2 * q]
            v = rlo[t + a, pl.ds(b, TALL)]
            if 2 * q + 1 < 9:
                a, b = taps[2 * q + 1]
                v = v + rhi[t + a, pl.ds(b, TALL)]
            patch[:, 128 * q : 128 * (q + 1)] = v.reshape(TALL * COLS, 128)
        mid[...] = jnp.dot(patch[...], we[...], preferred_element_type=F32)
        for y in range(TALL):
            v = mid[pl.ds(COLS * y, COLS)].astype(BF16)
            if 1 <= y <= ROWS:
                first[t, pl.ds(COLS * (y - 1), COLS)] = v
            h = silu_norm(v.astype(F32), g1_ref[...])
            if y == 0:
                h = h * has_up
            if y == TALL - 1:
                h = h * has_down
            put_row(h1, t, y, h)

    up = lax.rem(band + BANDS - 1, BANDS)
    down = lax.rem(band + 1, BANDS)

    def conv_step(source, weight, t):
        window = jnp.concatenate(
            [source[t, b : b + ROWS].reshape(CELLS, 3 * C) for b in range(3)], axis=1
        )
        outs = min(3, FRAMES - t)
        r = jnp.dot(window, weight[:, 0 : C * outs], preferred_element_type=F32)
        for k in range(outs):
            part = r[:, C * k : C * (k + 1)]
            if t == 0 or k == 2:
                acc[t + k] = part
            else:
                acc[t + k] += part

    for load in loads[9:12]:
        load.wait()
    halos = []
    for t in range(FRAMES):
        conv_step(h1, w1, t)
        for y in range(ROWS):
            put_row(h2, t, y + 1, silu_norm(acc[t, pl.ds(COLS * y, COLS)], g2_ref[...]))
        pair = []
        for side, (src, dst, to) in enumerate(((1, TALL - 1, up), (ROWS, 0, down))):
            pair.append(
                pltpu.make_async_remote_copy(
                    src_ref=h2.at[t, src, :, pl.ds(C, C)],
                    dst_ref=h2.at[t, dst, :, pl.ds(C, C)],
                    send_sem=hsend.at[t, side],
                    recv_sem=hrecv.at[t, side],
                    device_id=(seq, to),
                    device_id_type=MESH,
                )
            )
        for copy in pair:
            copy.start()
        halos.append(pair)

    for load in loads[12:15]:
        load.wait()
    edges = []
    for t in range(FRAMES):
        for copy in halos[t]:
            copy.wait_recv()
        put_row(h2, t, TALL - 1, h2[t, TALL - 1, :, C : 2 * C].astype(F32) * has_down)
        put_row(h2, t, 0, h2[t, 0, :, C : 2 * C].astype(F32) * has_up)
        conv_step(h2, w2, t)
        total = (acc[t] + first[t].astype(F32)).astype(BF16)
        s_ref[t + 2, 1 : ROWS + 1] = total.reshape(ROWS, COLS, C)
        pair = []
        for side, (src, dst, to) in enumerate(((1, TALL - 1, up), (ROWS, 0, down))):
            pair.append(
                pltpu.make_async_remote_copy(
                    src_ref=s_ref.at[t + 2, src],
                    dst_ref=s_ref.at[t + 2, dst],
                    send_sem=ssend.at[t, side],
                    recv_sem=srecv.at[t, side],
                    device_id=(seq, to),
                    device_id_type=MESH,
                )
            )
        for copy in pair:
            copy.start()
        edges.append(pair)

    loads[15].wait()
    for pair in edges:
        for copy in pair:
            copy.wait_recv()
    for t in range(FRAMES):
        s_ref[t + 2, 0] = (s_ref[t + 2, 0].astype(F32) * has_up).astype(BF16)
        s_ref[t + 2, TALL - 1] = (s_ref[t + 2, TALL - 1].astype(F32) * has_down).astype(BF16)
    for i in range(BLOCK):
        window = jnp.concatenate(
            [s_ref[BLOCK * half + i + a].reshape(TALL * COLS, C) for a in range(3)], axis=1
        )
        r = jnp.dot(window, wt[...], preferred_element_type=F32).astype(BF16)
        out_ref[2 * i] = r[:, 0:C].reshape(TALL, COLS, C)
        out_ref[2 * i + 1] = r[:, C : 2 * C].reshape(TALL, COLS, C)

    for push in pushes:
        push.wait_send()
    swap.wait_send()
    for pair in halos + edges:
        for copy in pair:
            copy.wait_send()


def stem(lat, arr, we, g1, w1, g2, w2, wt):
    vmem = pl.BlockSpec(memory_space=pltpu.VMEM)
    smem = pl.BlockSpec(memory_space=pltpu.SMEM)
    hbm = pl.BlockSpec(memory_space=pl.ANY)
    dma = pltpu.SemaphoreType.DMA
    return pl.pallas_call(
        stem_kernel,
        out_shape=jax.ShapeDtypeStruct((2 * BLOCK, TALL, COLS, C), BF16),
        in_specs=[vmem, smem, hbm, vmem, hbm, vmem, hbm, hbm],
        out_specs=vmem,
        scratch_shapes=[
            pltpu.VMEM((2 * BANDS, ROWS, COLS * LAT), BF16),
            pltpu.VMEM((2, 16, COLS * LAT), BF16),
            pltpu.VMEM((3, 32, COLS * LAT), F32),
            pltpu.VMEM((32, COLS, 768), BF16),
            pltpu.VMEM((6, 8, COLS, 128), BF16),
            pltpu.VMEM((6, 8, COLS, 128), BF16),
            pltpu.VMEM((TALL * COLS, 640), BF16),
            pltpu.VMEM((TALL * COLS, C), F32),
            pltpu.VMEM((FRAMES, CELLS, C), BF16),
            pltpu.VMEM((FRAMES, TALL, COLS, 3 * C), BF16),
            pltpu.VMEM((FRAMES, TALL, COLS, 3 * C), BF16),
            pltpu.VMEM((FRAMES, CELLS, C), F32),
            pltpu.VMEM((FRAMES + 2, TALL, COLS, C), BF16),
            pltpu.VMEM((640, C), BF16),
            pltpu.VMEM((9 * C, 3 * C), BF16),
            pltpu.VMEM((9 * C, 3 * C), BF16),
            pltpu.VMEM((3 * C, 2 * C), BF16),
            dma((16,)),
            dma((BANDS,)),
            dma((BANDS,)),
            dma((2,)),
            dma((FRAMES, 2)),
            dma((FRAMES, 2)),
            dma((FRAMES, 2)),
            dma((FRAMES, 2)),
        ],
        compiler_params=pltpu.CompilerParams(
            collective_id=0, has_side_effects=True, vmem_limit_bytes=56 * 2**20
        ),
        name="stem",
    )(lat, arr, we, g1, w1, g2, w2, wt)


def upsample_kernel(d_ref, w_ref, out_ref, wide, phase, low, high):
    @pl.when(pl.program_id(0) == 0)
    def _():
        spans = (((0,), (1, 2)), ((0, 1), (2,)))
        for py in range(2):
            for px in range(2):
                for dy in range(2):
                    for dx in range(2):
                        total = None
                        for ty in spans[py][dy]:
                            for tx in spans[px][dx]:
                                term = w_ref[3 * ty + tx].astype(F32)
                                total = term if total is None else total + term
                        at = (2 * dy + dx) * C
                        phase[2 * py + px, 0:CO, at : at + C] = total.astype(BF16)
        phase[:, CO:256] = jnp.zeros((4, 256 - CO, 4 * C), BF16)

    frames = d_ref.shape[0]
    for f in range(frames):
        for y in range(TALL):
            h = d_ref[f, y].astype(F32)
            left, right = shifted(h)
            wide[f, y, :, 0:C] = left.astype(BF16)
            wide[f, y, :, C : 2 * C] = d_ref[f, y]
            wide[f, y, :, 2 * C : 3 * C] = right.astype(BF16)
    for py in range(2):
        for px in range(2):
            window = jnp.concatenate(
                [
                    wide[:, py + dy : py + dy + ROWS, :, C * px : C * (px + 2)].reshape(
                        frames * CELLS, 2 * C
                    )
                    for dy in range(2)
                ],
                axis=1,
            )
            r = lax.dot_general(
                window,
                phase[2 * py + px],
                (((1,), (1,)), ((), ())),
                preferred_element_type=F32,
            )
            for f in range(frames):
                for y in range(ROWS):
                    at = (f * ROWS + y) * COLS
                    low[f, y, py, pl.ds(px, COLS, 2), :] = r[at : at + COLS, 0:128]
                    high[f, y, py, pl.ds(px, COLS, 2), :] = r[at : at + COLS, 128:256]
    for f in range(frames):
        for y in range(ROWS):
            for py in range(2):
                out_ref[f, 2 * y + py, :, 0:128] = low[f, y, py].astype(BF16)
                out_ref[f, 2 * y + py, :, 128:CO] = high[f, y, py, :, 0 : CO - 128].astype(BF16)


def upsample(doubled, w):
    frames = 2
    return pl.pallas_call(
        upsample_kernel,
        grid=(2 * BLOCK // frames,),
        out_shape=jax.ShapeDtypeStruct((2 * BLOCK, 2 * ROWS, 2 * COLS, CO), BF16),
        in_specs=[
            pl.BlockSpec((frames, TALL, COLS, C), lambda f: (f, 0, 0, 0)),
            pl.BlockSpec((9, CO, C), lambda f: (0, 0, 0)),
        ],
        out_specs=pl.BlockSpec((frames, 2 * ROWS, 2 * COLS, CO), lambda f: (f, 0, 0, 0)),
        scratch_shapes=[
            pltpu.VMEM((frames, TALL, COLS, 3 * C), BF16),
            pltpu.VMEM((4, 256, 4 * C), BF16),
            pltpu.VMEM((frames, ROWS, 2, 2 * COLS, 128), F32),
            pltpu.VMEM((frames, ROWS, 2, 2 * COLS, 128), F32),
        ],
        compiler_params=pltpu.CompilerParams(vmem_limit_bytes=48 * 2**20),
        name="upsample",
    )(doubled, w)


def local(
    transformer_latents,
    tile_arrangement,
    entry_conv_weight,
    first_norm_gain,
    first_conv_weight,
    second_norm_gain,
    second_conv_weight,
    temporal_upscale_weight,
    spatial_upscale_weight,
):
    doubled = stem(
        transformer_latents,
        tile_arrangement,
        entry_conv_weight.reshape(27 * LAT, C),
        first_norm_gain.reshape(1, C),
        first_conv_weight.reshape(3, 9 * C, C),
        second_norm_gain.reshape(1, C),
        second_conv_weight.reshape(3, 9 * C, C),
        temporal_upscale_weight.reshape(3 * C, 2 * C),
    )
    return upsample(
        doubled, jnp.transpose(spatial_upscale_weight, (0, 1, 3, 2)).reshape(9, CO, C)
    )


def solution(mesh):
    return jax.shard_map(
        local,
        mesh=mesh,
        in_specs=(P("seq", "tile", None), P("seq", None), P(), P(), P(), P(), P(), P(), P()),
        out_specs=P("seq", "tile", None, None),
        check_vma=False,
    )
```

```python
import functools

import jax
import jax.numpy as jnp
from jax import lax
from jax.experimental import pallas as pl
from jax.experimental.pallas import tpu as pltpu
from jax.sharding import PartitionSpec as P

EPS = 1e-06
MESH = pl.DeviceIdType.MESH
F32 = jnp.float32
BF16 = jnp.bfloat16

FRAMES = 4
BLOCK = 2
ROWS = 4
COLS = 64
LAT = 16
C = 384
CO = 192
BANDS = 16
TALL = ROWS + 2
CELLS = ROWS * COLS
PAIR = 2 * COLS


def silu_norm(v, gain):
    mean = jnp.sum(v * v, axis=-1, keepdims=True) * (1.0 / C)
    u = v * lax.rsqrt(mean + EPS) * gain
    return u / (1.0 + jnp.exp(-u))


def column(shape):
    return lax.broadcasted_iota(jnp.int32, shape, 0)


def shifted(h):
    col = column(h.shape)
    left = jnp.where(col == 0, 0.0, pltpu.roll(h, 1, 0))
    right = jnp.where(col == COLS - 1, 0.0, pltpu.roll(h, COLS - 1, 0))
    return left, right


def put_row(ref, t, y, h):
    left, right = shifted(h)
    ref[t, y, :, 0:C] = left.astype(BF16)
    ref[t, y, :, C : 2 * C] = h.astype(BF16)
    ref[t, y, :, 2 * C : 3 * C] = right.astype(BF16)


def stem_kernel(
    lat_ref,
    arr_ref,
    we_hbm,
    g1_ref,
    w1_hbm,
    g2_ref,
    w2_hbm,
    wt_hbm,
    out_ref,
    gath,
    lat4,
    late,
    lhs,
    rlo,
    rhi,
    patch,
    mid,
    first,
    h1,
    h2,
    acc,
    s_ref,
    we,
    w1,
    w2,
    wt,
    wsem,
    gsend,
    grecv,
    psem,
    hsend,
    hrecv,
    ssend,
    srecv,
):
    seq = lax.axis_index("seq")
    band = lax.axis_index("tile")
    half = lax.rem(seq, 2)
    mate = seq + 1 - 2 * half

    loads = []
    for p in range(9):
        loads.append(
            pltpu.make_async_copy(
                we_hbm.at[pl.ds(48 * p, 48)], we.at[pl.ds(64 * p, 48)], wsem.at[p]
            )
        )
    for k in range(3):
        loads.append(
            pltpu.make_async_copy(w1_hbm.at[2 - k], w1.at[:, pl.ds(k * C, C)], wsem.at[9 + k])
        )
    for k in range(3):
        loads.append(
            pltpu.make_async_copy(w2_hbm.at[2 - k], w2.at[:, pl.ds(k * C, C)], wsem.at[12 + k])
        )
    loads.append(pltpu.make_async_copy(wt_hbm, wt, wsem.at[15]))

    barrier = pltpu.get_barrier_semaphore()
    for d in range(1, BANDS):
        pl.semaphore_signal(
            barrier, inc=1, device_id=(seq, lax.rem(band + d, BANDS)), device_id_type=MESH
        )
    pl.semaphore_signal(barrier, inc=1, device_id=(mate, band), device_id_type=MESH)
    for load in loads:
        load.start()
    pl.semaphore_wait(barrier, BANDS)

    pushes = []
    for d in range(1, BANDS):
        pushes.append(
            pltpu.make_async_remote_copy(
                src_ref=lat_ref,
                dst_ref=gath.at[pl.ds(2 * band, 2)],
                send_sem=gsend.at[d],
                recv_sem=grecv.at[d],
                device_id=(seq, lax.rem(band + d, BANDS)),
                device_id_type=MESH,
            )
        )
    for push in pushes:
        push.start()
    gath[pl.ds(2 * band, 2)] = lat_ref[...]

    for p in range(9):
        we[pl.ds(64 * p + 48, 16)] = jnp.zeros((16, C), BF16)
    we[pl.ds(576, 64)] = jnp.zeros((64, C), BF16)
    rlo[0:2] = jnp.zeros((2, 8, COLS, 128), BF16)
    rhi[0:2] = jnp.zeros((2, 8, COLS, 128), BF16)
    s_ref[0:2] = jnp.zeros((2, TALL, COLS, C), BF16)
    spots = []
    for i in range(BLOCK):
        for o in (-1, 0, 1):
            target = i * BANDS + band + o
            spot = jnp.int32(0)
            for n in range(2 * BANDS):
                spot = jnp.where(arr_ref[0, n] == target, n, spot)
            spots.append(spot)

    for push in pushes:
        push.wait_recv()

    has_up = (band > 0).astype(F32)
    has_down = (band < BANDS - 1).astype(F32)
    picked = []
    for i in range(BLOCK):
        above = gath[spots[3 * i]].astype(F32) * has_up
        own = gath[spots[3 * i + 1]].astype(F32)
        below = gath[spots[3 * i + 2]].astype(F32) * has_down
        picked.append(jnp.concatenate([above[2:4], own, below[0:2]], axis=0))
    lat4[half] = jnp.concatenate(picked, axis=0).astype(BF16)
    swap = pltpu.make_async_remote_copy(
        src_ref=lat4.at[half],
        dst_ref=lat4.at[half],
        send_sem=psem.at[0],
        recv_sem=psem.at[1],
        device_id=(mate, band),
        device_id_type=MESH,
    )
    swap.start()

    spread = (
        lax.rem(lax.broadcasted_iota(jnp.int32, (16, COLS * LAT), 1), 256) // LAT
        == lax.broadcasted_iota(jnp.int32, (16, COLS * LAT), 0)
    ).astype(F32)
    kk = lax.broadcasted_iota(jnp.int32, (768, 256), 0)
    nn = lax.broadcasted_iota(jnp.int32, (768, 256), 1)
    want = jnp.where(nn < 128, nn, nn - 128 - 64)
    place = (
        (want >= 0)
        & (want < 48)
        & (want // LAT == kk // 256)
        & (lax.rem(want, LAT) == lax.rem(kk, LAT))
    )
    place = place.astype(F32).astype(BF16)

    def relayout(block):
        lat = lat4[block].astype(F32)
        lane = lax.broadcasted_iota(jnp.int32, lat.shape, 1)
        late[0] = jnp.where(lane < LAT, 0.0, pltpu.roll(lat, LAT, 1))
        late[1] = lat
        late[2] = jnp.where(lane >= (COLS - 1) * LAT, 0.0, pltpu.roll(lat, (COLS - 1) * LAT, 1))

        @pl.loop(0, 16)
        def _(r):
            for e in range(3):
                row = late[e, pl.ds(r, 1), :]
                full = (jnp.broadcast_to(row, (16, COLS * LAT)) * spread).astype(BF16)
                for g in range(4):
                    lhs[r, pl.ds(16 * g, 16), 256 * e : 256 * (e + 1)] = full[
                        :, 256 * g : 256 * (g + 1)
                    ]

        @pl.loop(0, 2)
        def _(i):
            r = jnp.dot(
                lhs[pl.ds(8 * i, 8)].reshape(8 * COLS, 768), place, preferred_element_type=F32
            ).astype(BF16)
            t = 2 * block + i
            rlo[t + 2] = r[:, 0:128].reshape(8, COLS, 128)
            rhi[t + 2] = r[:, 128:256].reshape(8, COLS, 128)

    relayout(half)
    swap.wait_recv()
    relayout(1 - half)

    for load in loads[:9]:
        load.wait()

    @pl.loop(0, 4)
    def _(t):
        taps = [(a, b) for a in range(3) for b in range(3)]
        for q in range(5):
            a, b = taps[2 * q]
            v = rlo[t + a, pl.ds(b, TALL)]
            if 2 * q + 1 < 9:
                a, b = taps[2 * q + 1]
                v = v + rhi[t + a, pl.ds(b, TALL)]
            patch[:, 128 * q : 128 * (q + 1)] = v.reshape(TALL * COLS, 128)
        mid[...] = jnp.dot(patch[...], we[...], preferred_element_type=F32)
        for y in range(TALL):
            v = mid[pl.ds(COLS * y, COLS)].astype(BF16)
            if 1 <= y <= ROWS:
                first[t, pl.ds(COLS * (y - 1), COLS)] = v
            h = silu_norm(v.astype(F32), g1_ref[...])
            if y == 0:
                h = h * has_up
            if y == TALL - 1:
                h = h * has_down
            put_row(h1, t, y, h)

    up = lax.rem(band + BANDS - 1, BANDS)
    down = lax.rem(band + 1, BANDS)

    def window(source, t, edge):
        rows = (0, 3) if edge else (1, 2)
        return jnp.concatenate(
            [
                jnp.concatenate([source[t + i, y + b] for b in range(3)], axis=1)
                for i in range(2)
                for y in rows
            ],
            axis=0,
        )

    def early(source, weight, edge):
        r = jnp.dot(window(source, 0, edge), weight[...], preferred_element_type=F32)
        acc[0] = r[0:PAIR, 0:C]
        acc[1] = r[0:PAIR, C : 2 * C] + r[PAIR:, 0:C]
        acc[2] = r[0:PAIR, 2 * C :] + r[PAIR:, C : 2 * C]
        acc[3] = r[PAIR:, 2 * C :]

    def late_part(source, weight, edge):
        r = jnp.dot(window(source, 2, edge), weight[:, 0 : 2 * C], preferred_element_type=F32)
        acc[2] += r[0:PAIR, 0:C]
        acc[3] += r[0:PAIR, C:] + r[PAIR:, 0:C]

    def activate(t, edge):
        for i in range(2):
            for k, y in enumerate((0, 3) if edge else (1, 2)):
                put_row(
                    h2,
                    t + i,
                    y + 1,
                    silu_norm(acc[t + i, pl.ds(COLS * k, COLS)], g2_ref[...]),
                )

    def finish(t, edge):
        for i in range(2):
            for k, y in enumerate((0, 3) if edge else (1, 2)):
                total = acc[t + i, pl.ds(COLS * k, COLS)] + first[
                    t + i, pl.ds(COLS * y, COLS)
                ].astype(F32)
                s_ref[t + i + 2, y + 1] = total.astype(BF16)

    def push_rows(ref, t, lanes, sends, recvs):
        pair = []
        for side, (src, dst, to) in enumerate(((1, TALL - 1, up), (ROWS, 0, down))):
            pair.append(
                pltpu.make_async_remote_copy(
                    src_ref=ref.at[pl.ds(t, 2), src, :, lanes],
                    dst_ref=ref.at[pl.ds(t, 2), dst, :, lanes],
                    send_sem=sends.at[t // 2, side],
                    recv_sem=recvs.at[t // 2, side],
                    device_id=(seq, to),
                    device_id_type=MESH,
                )
            )
        for copy in pair:
            copy.start()
        return pair

    for load in loads[9:12]:
        load.wait()
    middle = pl.ds(C, C)
    early(h1, w1, True)
    activate(0, True)
    halos = [push_rows(h2, 0, middle, hsend, hrecv)]
    late_part(h1, w1, True)
    activate(2, True)
    halos.append(push_rows(h2, 2, middle, hsend, hrecv))
    early(h1, w1, False)
    activate(0, False)
    late_part(h1, w1, False)
    activate(2, False)

    for load in loads[12:15]:
        load.wait()

    def take_halo(t):
        for copy in halos[t // 2]:
            copy.wait_recv()
        for i in range(2):
            put_row(h2, t + i, 0, h2[t + i, 0, :, C : 2 * C].astype(F32) * has_up)
            put_row(
                h2, t + i, TALL - 1, h2[t + i, TALL - 1, :, C : 2 * C].astype(F32) * has_down
            )

    whole = pl.ds(0, C)
    take_halo(0)
    early(h2, w2, True)
    finish(0, True)
    edges = [push_rows(s_ref.at[pl.ds(2, 4)], 0, whole, ssend, srecv)]
    take_halo(2)
    late_part(h2, w2, True)
    finish(2, True)
    edges.append(push_rows(s_ref.at[pl.ds(2, 4)], 2, whole, ssend, srecv))
    early(h2, w2, False)
    finish(0, False)
    late_part(h2, w2, False)
    finish(2, False)

    loads[15].wait()

    def double(rows):
        cells = len(rows) * COLS
        stacked = jnp.concatenate(
            [
                jnp.concatenate(
                    [s_ref[BLOCK * half + i + a, y] for a in range(3)], axis=1
                )
                for i in range(BLOCK)
                for y in rows
            ],
            axis=0,
        )
        r = jnp.dot(stacked, wt[...], preferred_element_type=F32).astype(BF16)
        for i in range(BLOCK):
            for k, y in enumerate(rows):
                at = i * cells + k * COLS
                out_ref[2 * i, y] = r[at : at + COLS, 0:C]
                out_ref[2 * i + 1, y] = r[at : at + COLS, C : 2 * C]

    double(range(1, ROWS + 1))
    for pair in edges:
        for copy in pair:
            copy.wait_recv()
    for t in range(FRAMES):
        s_ref[t + 2, 0] = (s_ref[t + 2, 0].astype(F32) * has_up).astype(BF16)
        s_ref[t + 2, TALL - 1] = (s_ref[t + 2, TALL - 1].astype(F32) * has_down).astype(BF16)
    double((0, TALL - 1))

    for push in pushes:
        push.wait_send()
    swap.wait_send()
    for pair in halos + edges:
        for copy in pair:
            copy.wait_send()


def stem(lat, arr, we, g1, w1, g2, w2, wt):
    vmem = pl.BlockSpec(memory_space=pltpu.VMEM)
    smem = pl.BlockSpec(memory_space=pltpu.SMEM)
    hbm = pl.BlockSpec(memory_space=pl.ANY)
    dma = pltpu.SemaphoreType.DMA
    return pl.pallas_call(
        stem_kernel,
        out_shape=jax.ShapeDtypeStruct((2 * BLOCK, TALL, COLS, C), BF16),
        in_specs=[vmem, smem, hbm, vmem, hbm, vmem, hbm, hbm],
        out_specs=vmem,
        scratch_shapes=[
            pltpu.VMEM((2 * BANDS, ROWS, COLS * LAT), BF16),
            pltpu.VMEM((2, 16, COLS * LAT), BF16),
            pltpu.VMEM((3, 16, COLS * LAT), F32),
            pltpu.VMEM((16, COLS, 768), BF16),
            pltpu.VMEM((6, 8, COLS, 128), BF16),
            pltpu.VMEM((6, 8, COLS, 128), BF16),
            pltpu.VMEM((TALL * COLS, 640), BF16),
            pltpu.VMEM((TALL * COLS, C), F32),
            pltpu.VMEM((FRAMES, CELLS, C), BF16),
            pltpu.VMEM((FRAMES, TALL, COLS, 3 * C), BF16),
            pltpu.VMEM((FRAMES, TALL, COLS, 3 * C), BF16),
            pltpu.VMEM((FRAMES, PAIR, C), F32),
            pltpu.VMEM((FRAMES + 2, TALL, COLS, C), BF16),
            pltpu.VMEM((640, C), BF16),
            pltpu.VMEM((9 * C, 3 * C), BF16),
            pltpu.VMEM((9 * C, 3 * C), BF16),
            pltpu.VMEM((3 * C, 2 * C), BF16),
            dma((16,)),
            dma((BANDS,)),
            dma((BANDS,)),
            dma((2,)),
            dma((2, 2)),
            dma((2, 2)),
            dma((2, 2)),
            dma((2, 2)),
        ],
        compiler_params=pltpu.CompilerParams(
            collective_id=0, has_side_effects=True, vmem_limit_bytes=56 * 2**20
        ),
        name="stem",
    )(lat, arr, we, g1, w1, g2, w2, wt)


def upsample_kernel(d_ref, w_ref, out_ref, wide, phase, low, high):
    @pl.when(pl.program_id(0) == 0)
    def _():
        spans = (((0,), (1, 2)), ((0, 1), (2,)))
        for py in range(2):
            for px in range(2):
                for dy in range(2):
                    for dx in range(2):
                        total = None
                        for ty in spans[py][dy]:
                            for tx in spans[px][dx]:
                                term = w_ref[3 * ty + tx].astype(F32)
                                total = term if total is None else total + term
                        at = (2 * dy + dx) * C
                        phase[2 * py + px, 0:CO, at : at + C] = total.astype(BF16)
        phase[:, CO:256] = jnp.zeros((4, 256 - CO, 4 * C), BF16)

    frames = d_ref.shape[0]
    for f in range(frames):
        for y in range(TALL):
            h = d_ref[f, y].astype(F32)
            left, right = shifted(h)
            wide[f, y, :, 0:C] = left.astype(BF16)
            wide[f, y, :, C : 2 * C] = d_ref[f, y]
            wide[f, y, :, 2 * C : 3 * C] = right.astype(BF16)
    for py in range(2):
        for px in range(2):
            window = jnp.concatenate(
                [
                    wide[:, py + dy : py + dy + ROWS, :, C * px : C * (px + 2)].reshape(
                        frames * CELLS, 2 * C
                    )
                    for dy in range(2)
                ],
                axis=1,
            )
            r = lax.dot_general(
                window,
                phase[2 * py + px],
                (((1,), (1,)), ((), ())),
                preferred_element_type=F32,
            )
            for f in range(frames):
                for y in range(ROWS):
                    at = (f * ROWS + y) * COLS
                    low[f, y, py, pl.ds(px, COLS, 2), :] = r[at : at + COLS, 0:128]
                    high[f, y, py, pl.ds(px, COLS, 2), :] = r[at : at + COLS, 128:256]
    for f in range(frames):
        for y in range(ROWS):
            for py in range(2):
                out_ref[f, 2 * y + py, 0:128] = low[f, y, py].T.astype(BF16)
                out_ref[f, 2 * y + py, 128:CO] = high[f, y, py].T[0 : CO - 128].astype(BF16)


def upsample(doubled, w):
    frames = 2
    return pl.pallas_call(
        upsample_kernel,
        grid=(2 * BLOCK // frames,),
        out_shape=jax.ShapeDtypeStruct((2 * BLOCK, 2 * ROWS, CO, 2 * COLS), BF16),
        in_specs=[
            pl.BlockSpec((frames, TALL, COLS, C), lambda f: (f, 0, 0, 0)),
            pl.BlockSpec((9, CO, C), lambda f: (0, 0, 0)),
        ],
        out_specs=pl.BlockSpec((frames, 2 * ROWS, CO, 2 * COLS), lambda f: (f, 0, 0, 0)),
        scratch_shapes=[
            pltpu.VMEM((frames, TALL, COLS, 3 * C), BF16),
            pltpu.VMEM((4, 256, 4 * C), BF16),
            pltpu.VMEM((frames, ROWS, 2, 2 * COLS, 128), F32),
            pltpu.VMEM((frames, ROWS, 2, 2 * COLS, 128), F32),
        ],
        compiler_params=pltpu.CompilerParams(vmem_limit_bytes=60 * 2**20),
        name="upsample",
    )(doubled, w)


def local(
    transformer_latents,
    tile_arrangement,
    entry_conv_weight,
    first_norm_gain,
    first_conv_weight,
    second_norm_gain,
    second_conv_weight,
    temporal_upscale_weight,
    spatial_upscale_weight,
):
    doubled = stem(
        transformer_latents,
        tile_arrangement,
        entry_conv_weight.reshape(27 * LAT, C),
        first_norm_gain,
        first_conv_weight.reshape(3, 9 * C, C),
        second_norm_gain,
        second_conv_weight.reshape(3, 9 * C, C),
        temporal_upscale_weight.reshape(3 * C, 2 * C),
    )
    decoded = upsample(
        doubled, jnp.transpose(spatial_upscale_weight, (0, 1, 3, 2)).reshape(9, CO, C)
    )
    return jnp.transpose(decoded, (0, 1, 3, 2))


def solution(mesh):
    return jax.shard_map(
        local,
        mesh=mesh,
        in_specs=(P("seq", "tile", None), P("seq", None), P(), P(), P(), P(), P(), P(), P()),
        out_specs=P("seq", "tile", None, None),
        check_vma=False,
    )
```

```python
import functools

import jax
import jax.numpy as jnp
from jax import lax
from jax.experimental import pallas as pl
from jax.experimental.pallas import tpu as pltpu
from jax.sharding import PartitionSpec as P

EPS = 1e-06
MESH = pl.DeviceIdType.MESH
F32 = jnp.float32
BF16 = jnp.bfloat16

FRAMES = 4
BLOCK = 2
ROWS = 4
COLS = 64
HALF = COLS // 2
LAT = 16
C = 384
CO = 192
BANDS = 16
TALL = ROWS + 2


def silu_norm(v, gain):
    mean = jnp.sum(v * v, axis=-1, keepdims=True) * (1.0 / C)
    u = v * lax.rsqrt(mean + EPS) * gain
    return u / (1.0 + jnp.exp(-u))


def before(odd):
    row = lax.broadcasted_iota(jnp.int32, odd.shape, 0)
    return jnp.where(row == 0, 0.0, pltpu.roll(odd, 1, 0))


def after(even):
    row = lax.broadcasted_iota(jnp.int32, even.shape, 0)
    return jnp.where(row == HALF - 1, 0.0, pltpu.roll(even, HALF - 1, 0))


def put_row(ref, t, y, even, odd):
    ref[t, y, 0] = (before(odd) - odd).astype(BF16)
    ref[t, y, 1] = (even + odd).astype(BF16)
    ref[t, y, 2] = (odd - even).astype(BF16)
    ref[t, y, 3] = (even - after(even)).astype(BF16)


def start_weights(w_hbm, u, sems):
    copies = []
    for a in range(3):
        for e, slot in enumerate((0, 1, 3)):
            copies.append(
                pltpu.make_async_copy(
                    w_hbm.at[a, :, e],
                    u.at[slot, :, :, pl.ds((2 - a) * C, C)],
                    sems.at[3 * a + e],
                )
            )
    return copies


def combine_weights(u):
    @pl.loop(0, 3 * (C // 16))
    def _(i):
        b, r = i // (C // 16), 16 * lax.rem(i, C // 16)
        rows = pl.ds(pl.multiple_of(r, 16), 16)
        outer = (u[0, b, rows].astype(F32) + u[3, b, rows].astype(F32)) * 0.5
        inner = u[1, b, rows].astype(F32) * 0.5
        u[1, b, rows] = (outer + inner).astype(BF16)
        u[2, b, rows] = (outer - inner).astype(BF16)


def windows(source, t, frames, k, rows):
    return jnp.concatenate(
        [
            jnp.concatenate([source[t + i, y + b, k] for b in range(3)], axis=1)
            for i in range(frames)
            for y in rows
        ],
        axis=0,
    )


def conv(source, u, acc, rows):
    n = HALF * len(rows)
    for k in range(4):
        weight = u[k].reshape(3 * C, 3 * C)
        if len(rows) == 1:
            r = jnp.dot(windows(source, 0, 4, k, rows), weight, preferred_element_type=F32)
            q = [r[n * i : n * (i + 1)] for i in range(4)]
        else:
            r = jnp.dot(windows(source, 0, 2, k, rows), weight, preferred_element_type=F32)
            q = [r[0:n], r[n:]]
            r = jnp.dot(
                windows(source, 2, 2, k, rows), weight[:, 0 : 2 * C], preferred_element_type=F32
            )
            q += [r[0:n], r[n:]]
        for t in range(FRAMES):
            part = q[t][:, 0:C]
            for back in range(1, min(t, 2) + 1):
                part = part + q[t - back][:, back * C : (back + 1) * C]
            if k == 0:
                acc[t, 0, 0:n] = part
            elif k == 1:
                acc[t, 0, 0:n] += part
                acc[t, 1, 0:n] = part
            elif k == 2:
                acc[t, 0, 0:n] += part
                acc[t, 1, 0:n] -= part
            else:
                acc[t, 1, 0:n] -= part


def stem_kernel(
    lat_ref,
    arr_ref,
    we_hbm,
    g1_ref,
    w1_hbm,
    g2_ref,
    w2_hbm,
    wt_hbm,
    out_ref,
    gath,
    lat4,
    late,
    lhs,
    rlo,
    rhi,
    patch,
    mid,
    first,
    h1,
    h2,
    acc,
    s_ref,
    slow_out,
    slow_in,
    fast_out,
    fast_in,
    we,
    u1,
    u2,
    wt,
    wsem,
    gsend,
    grecv,
    psem,
    hsend,
    hrecv,
    ssend,
    srecv,
):
    seq = lax.axis_index("seq")
    band = lax.axis_index("tile")
    half = lax.rem(seq, 2)
    mate = seq + 1 - 2 * half

    odd_band = lax.rem(band, 2)

    loads1 = start_weights(w1_hbm, u1, wsem.at[pl.ds(0, 9)])
    loads2 = start_weights(w2_hbm, u2, wsem.at[pl.ds(9, 9)])
    loads0 = []
    for p in range(9):
        loads0.append(
            pltpu.make_async_copy(
                we_hbm.at[pl.ds(48 * p, 48)], we.at[pl.ds(64 * p, 48)], wsem.at[18 + p]
            )
        )
    load_wt = pltpu.make_async_copy(wt_hbm, wt, wsem.at[27])

    barrier = pltpu.get_barrier_semaphore()
    for d in range(1, BANDS):
        pl.semaphore_signal(
            barrier, inc=1, device_id=(seq, lax.rem(band + d, BANDS)), device_id_type=MESH
        )
    pl.semaphore_signal(barrier, inc=1, device_id=(mate, band), device_id_type=MESH)
    for load in loads1 + loads0 + loads2 + [load_wt]:
        load.start()
    pl.semaphore_wait(barrier, BANDS)

    pushes = []
    for d in range(1, BANDS):
        pushes.append(
            pltpu.make_async_remote_copy(
                src_ref=lat_ref,
                dst_ref=gath.at[pl.ds(2 * band, 2)],
                send_sem=gsend.at[d],
                recv_sem=grecv.at[d],
                device_id=(seq, lax.rem(band + d, BANDS)),
                device_id_type=MESH,
            )
        )
    for push in pushes:
        push.start()
    gath[pl.ds(2 * band, 2)] = lat_ref[...]

    for p in range(9):
        we[pl.ds(64 * p + 48, 16)] = jnp.zeros((16, C), BF16)
    we[pl.ds(576, 64)] = jnp.zeros((64, C), BF16)
    rlo[0:2] = jnp.zeros((2, 8, COLS, 128), BF16)
    rhi[0:2] = jnp.zeros((2, 8, COLS, 128), BF16)
    s_ref[0:2] = jnp.zeros((2, TALL, COLS, C), BF16)
    spots = []
    for i in range(BLOCK):
        for o in (-1, 0, 1):
            target = i * BANDS + band + o
            spot = jnp.int32(0)
            for n in range(2 * BANDS):
                spot = jnp.where(arr_ref[0, n] == target, n, spot)
            spots.append(spot)

    for load in loads1:
        load.wait()
    combine_weights(u1)

    for push in pushes:
        push.wait_recv()

    has_up = (band > 0).astype(F32)
    has_down = (band < BANDS - 1).astype(F32)
    picked = []
    for i in range(BLOCK):
        above = gath[spots[3 * i]].astype(F32) * has_up
        own = gath[spots[3 * i + 1]].astype(F32)
        below = gath[spots[3 * i + 2]].astype(F32) * has_down
        picked.append(jnp.concatenate([above[2:4], own, below[0:2]], axis=0))
    lat4[half] = jnp.concatenate(picked, axis=0).astype(BF16)
    swap = pltpu.make_async_remote_copy(
        src_ref=lat4.at[half],
        dst_ref=lat4.at[half],
        send_sem=psem.at[0],
        recv_sem=psem.at[1],
        device_id=(mate, band),
        device_id_type=MESH,
    )
    swap.start()

    place_of = lax.broadcasted_iota(jnp.int32, (16, COLS * LAT), 0)
    column_of = 2 * lax.rem(place_of, 8) + place_of // 8
    spread = (
        lax.rem(lax.broadcasted_iota(jnp.int32, (16, COLS * LAT), 1), 256) // LAT == column_of
    ).astype(F32)
    kk = lax.broadcasted_iota(jnp.int32, (768, 256), 0)
    nn = lax.broadcasted_iota(jnp.int32, (768, 256), 1)
    want = jnp.where(nn < 128, nn, nn - 128 - 64)
    place = (
        (want >= 0)
        & (want < 48)
        & (want // LAT == kk // 256)
        & (lax.rem(want, LAT) == lax.rem(kk, LAT))
    )
    place = place.astype(F32).astype(BF16)

    def relayout(block):
        lat = lat4[block].astype(F32)
        lane = lax.broadcasted_iota(jnp.int32, lat.shape, 1)
        late[0] = jnp.where(lane < LAT, 0.0, pltpu.roll(lat, LAT, 1))
        late[1] = lat
        late[2] = jnp.where(lane >= (COLS - 1) * LAT, 0.0, pltpu.roll(lat, (COLS - 1) * LAT, 1))

        @pl.loop(0, 16)
        def _(r):
            for e in range(3):
                row = late[e, pl.ds(r, 1), :]
                full = (jnp.broadcast_to(row, (16, COLS * LAT)) * spread).astype(BF16)
                for g in range(4):
                    lhs[r, pl.ds(16 * g, 16), 256 * e : 256 * (e + 1)] = full[
                        :, 256 * g : 256 * (g + 1)
                    ]

        @pl.loop(0, 2)
        def _(i):
            r = jnp.dot(
                lhs[pl.ds(8 * i, 8)].reshape(8 * COLS, 768), place, preferred_element_type=F32
            )
            r = jnp.concatenate(
                [
                    r[at : at + 8]
                    for y in range(8)
                    for par in range(2)
                    for at in range(y * COLS + 8 * par, (y + 1) * COLS, 16)
                ],
                axis=0,
            ).astype(BF16)
            t = 2 * block + i
            rlo[t + 2] = r[:, 0:128].reshape(8, COLS, 128)
            rhi[t + 2] = r[:, 128:256].reshape(8, COLS, 128)

    relayout(half)
    for load in loads2:
        load.wait()
    combine_weights(u2)
    swap.wait_recv()
    relayout(1 - half)

    for load in loads0:
        load.wait()

    @pl.loop(0, 4)
    def _(t):
        taps = [(a, b) for a in range(3) for b in range(3)]
        for q in range(5):
            a, b = taps[2 * q]
            v = rlo[t + a, pl.ds(b, TALL)]
            if 2 * q + 1 < 9:
                a, b = taps[2 * q + 1]
                v = v + rhi[t + a, pl.ds(b, TALL)]
            patch[:, 128 * q : 128 * (q + 1)] = v.reshape(TALL * COLS, 128)
        mid[...] = jnp.dot(patch[...], we[...], preferred_element_type=F32)
        for y in range(TALL):
            v = mid[pl.ds(COLS * y, COLS)].astype(BF16)
            if 1 <= y <= ROWS:
                first[t, y - 1] = v
            h = silu_norm(v.astype(F32), g1_ref[...])
            if y == 0:
                h = h * has_up
            if y == TALL - 1:
                h = h * has_down
            put_row(h1, t, y, h[0:HALF], h[HALF:])

    far = lax.rem(band + BANDS - 1 + 2 * odd_band, BANDS)
    near = band + 1 - 2 * odd_band
    far_inside = jnp.where(odd_band == 0, has_up, has_down)
    far_row = 3 * odd_band
    near_row = 3 - far_row
    far_halo = 5 * odd_band
    near_halo = 5 - far_halo
    others = [1 - odd_band + i for i in range(3)]

    def push_to(src, dst, to, send, recv):
        copy = pltpu.make_async_remote_copy(
            src_ref=src,
            dst_ref=dst,
            send_sem=send,
            recv_sem=recv,
            device_id=(seq, to),
            device_id_type=MESH,
        )
        copy.start()
        return copy

    def activate(t, k, y, out=None):
        rows = pl.ds(HALF * k, HALF)
        even = silu_norm(acc[t, 0, rows], g2_ref[...])
        odd = silu_norm(acc[t, 1, rows], g2_ref[...])
        put_row(h2, t, y + 1, even, odd)
        if out is not None:
            out[t, 0:HALF] = even.astype(BF16)
            out[t, HALF:] = odd.astype(BF16)

    conv(h1, u1, acc, [far_row])
    for t in range(FRAMES):
        activate(t, 0, far_row, slow_out)
    halos = [push_to(slow_out, slow_in, far, hsend.at[0], hrecv.at[0])]
    conv(h1, u1, acc, others)
    for t in range(FRAMES):
        for k in range(3):
            activate(t, k, others[k])
    for t in range(FRAMES):
        rows = pl.ds(pl.multiple_of(2 * HALF * (1 - odd_band), HALF), HALF)
        fast_out[t, 0:HALF] = silu_norm(acc[t, 0, rows], g2_ref[...]).astype(BF16)
        fast_out[t, HALF:] = silu_norm(acc[t, 1, rows], g2_ref[...]).astype(BF16)
    halos.append(push_to(fast_out, fast_in, near, hsend.at[1], hrecv.at[1]))

    def finish(t, k, y):
        rows = pl.ds(HALF * k, HALF)
        for par in range(2):
            cols = pl.ds(HALF * par, HALF)
            total = acc[t, par, rows] + first[t, y, cols].astype(F32)
            s_ref[t + 2, y + 1, cols] = total.astype(BF16)

    halos[0].wait_recv()
    for t in range(FRAMES):
        h = slow_in[t].astype(F32) * far_inside
        put_row(h2, t, far_halo, h[0:HALF], h[HALF:])
    conv(h2, u2, acc, [far_row])
    for t in range(FRAMES):
        finish(t, 0, far_row)
    frames = pl.ds(2, FRAMES)
    edges = [
        push_to(
            s_ref.at[frames, far_row + 1],
            s_ref.at[frames, 5 - far_halo],
            far,
            ssend.at[0],
            srecv.at[0],
        )
    ]
    halos[1].wait_recv()
    for t in range(FRAMES):
        h = fast_in[t].astype(F32)
        put_row(h2, t, near_halo, h[0:HALF], h[HALF:])
    conv(h2, u2, acc, others)
    for t in range(FRAMES):
        for k in range(3):
            finish(t, k, others[k])
    edges.append(
        push_to(
            s_ref.at[frames, near_row + 1],
            s_ref.at[frames, 5 - near_halo],
            near,
            ssend.at[1],
            srecv.at[1],
        )
    )

    load_wt.wait()

    def double(rows):
        cells = len(rows) * COLS
        stacked = jnp.concatenate(
            [
                jnp.concatenate(
                    [s_ref[BLOCK * half + i + a, y] for a in range(3)], axis=1
                )
                for i in range(BLOCK)
                for y in rows
            ],
            axis=0,
        )
        r = jnp.dot(stacked, wt[...], preferred_element_type=F32).astype(BF16)
        for i in range(BLOCK):
            for k, y in enumerate(rows):
                at = i * cells + k * COLS
                out_ref[2 * i, y] = r[at : at + COLS, 0:C]
                out_ref[2 * i + 1, y] = r[at : at + COLS, C : 2 * C]

    double(range(1, ROWS + 1))
    for copy in edges:
        copy.wait_recv()
    for t in range(FRAMES):
        s_ref[t + 2, far_halo] = (s_ref[t + 2, far_halo].astype(F32) * far_inside).astype(BF16)
    double((0, TALL - 1))

    for push in pushes:
        push.wait_send()
    swap.wait_send()
    for copy in halos + edges:
        copy.wait_send()


def stem(lat, arr, we, g1, w1, g2, w2, wt):
    vmem = pl.BlockSpec(memory_space=pltpu.VMEM)
    smem = pl.BlockSpec(memory_space=pltpu.SMEM)
    hbm = pl.BlockSpec(memory_space=pl.ANY)
    dma = pltpu.SemaphoreType.DMA
    return pl.pallas_call(
        stem_kernel,
        out_shape=jax.ShapeDtypeStruct((2 * BLOCK, TALL, COLS, C), BF16),
        in_specs=[vmem, smem, hbm, vmem, hbm, vmem, hbm, hbm],
        out_specs=vmem,
        scratch_shapes=[
            pltpu.VMEM((2 * BANDS, ROWS, COLS * LAT), BF16),
            pltpu.VMEM((2, 16, COLS * LAT), BF16),
            pltpu.VMEM((3, 16, COLS * LAT), F32),
            pltpu.VMEM((16, COLS, 768), BF16),
            pltpu.VMEM((6, 8, COLS, 128), BF16),
            pltpu.VMEM((6, 8, COLS, 128), BF16),
            pltpu.VMEM((TALL * COLS, 640), BF16),
            pltpu.VMEM((TALL * COLS, C), F32),
            pltpu.VMEM((FRAMES, ROWS, COLS, C), BF16),
            pltpu.VMEM((FRAMES, TALL, 4, HALF, C), BF16),
            pltpu.VMEM((FRAMES, TALL, 4, HALF, C), BF16),
            pltpu.VMEM((FRAMES, 2, 3 * HALF, C), F32),
            pltpu.VMEM((FRAMES + 2, TALL, COLS, C), BF16),
            pltpu.VMEM((FRAMES, COLS, C), BF16),
            pltpu.VMEM((FRAMES, COLS, C), BF16),
            pltpu.VMEM((FRAMES, COLS, C), BF16),
            pltpu.VMEM((FRAMES, COLS, C), BF16),
            pltpu.VMEM((640, C), BF16),
            pltpu.VMEM((4, 3, C, 3 * C), BF16),
            pltpu.VMEM((4, 3, C, 3 * C), BF16),
            pltpu.VMEM((3 * C, 2 * C), BF16),
            dma((28,)),
            dma((BANDS,)),
            dma((BANDS,)),
            dma((2,)),
            dma((2,)),
            dma((2,)),
            dma((2,)),
            dma((2,)),
        ],
        compiler_params=pltpu.CompilerParams(
            collective_id=0, has_side_effects=True, vmem_limit_bytes=56 * 2**20
        ),
        name="stem",
    )(lat, arr, we, g1, w1, g2, w2, wt)


def upsample_kernel(d_ref, w_ref, out_ref, wide, phase, low, high):
    @pl.when(pl.program_id(0) == 0)
    def _():
        spans = (((0,), (1, 2)), ((0, 1), (2,)))
        for py in range(2):
            for px in range(2):
                for dy in range(2):
                    for dx in range(2):
                        total = None
                        for ty in spans[py][dy]:
                            for tx in spans[px][dx]:
                                term = w_ref[3 * ty + tx].astype(F32)
                                total = term if total is None else total + term
                        at = (2 * dy + dx) * C
                        phase[2 * py + px, 0:CO, at : at + C] = total.astype(BF16)
        phase[:, CO:256] = jnp.zeros((4, 256 - CO, 4 * C), BF16)

    frames = d_ref.shape[0]
    for f in range(frames):
        for y in range(TALL):
            even, odd = d_ref[f, y, 0:HALF], d_ref[f, y, HALF:]
            wide[f, y, :, 0:C] = before(odd.astype(F32)).astype(BF16)
            wide[f, y, :, C : 2 * C] = even
            wide[f, y, :, 2 * C : 3 * C] = odd
            wide[f, y, :, 3 * C : 4 * C] = after(even.astype(F32)).astype(BF16)
    for py in range(2):
        for px in range(2):
            window = jnp.concatenate(
                [
                    jnp.concatenate(
                        [
                            wide[f, y + py + dy, :, C * (px + par) : C * (px + par + 2)]
                            for dy in range(2)
                        ],
                        axis=1,
                    )
                    for f in range(frames)
                    for y in range(ROWS)
                    for par in range(2)
                ],
                axis=0,
            )
            r = lax.dot_general(
                window,
                phase[2 * py + px],
                (((1,), (1,)), ((), ())),
                preferred_element_type=F32,
            )
            for f in range(frames):
                for y in range(ROWS):
                    for par in range(2):
                        at = ((f * ROWS + y) * 2 + par) * HALF
                        cols = pl.ds(2 * par + px, HALF, 4)
                        low[f, y, py, cols, :] = r[at : at + HALF, 0:128]
                        high[f, y, py, cols, :] = r[at : at + HALF, 128:256]
    for f in range(frames):
        for y in range(ROWS):
            for py in range(2):
                out_ref[f, 2 * y + py, 0:128] = low[f, y, py].T.astype(BF16)
                out_ref[f, 2 * y + py, 128:CO] = high[f, y, py].T[0 : CO - 128].astype(BF16)


def upsample(doubled, w):
    frames = 2
    return pl.pallas_call(
        upsample_kernel,
        grid=(2 * BLOCK // frames,),
        out_shape=jax.ShapeDtypeStruct((2 * BLOCK, 2 * ROWS, CO, 2 * COLS), BF16),
        in_specs=[
            pl.BlockSpec((frames, TALL, COLS, C), lambda f: (f, 0, 0, 0)),
            pl.BlockSpec((9, CO, C), lambda f: (0, 0, 0)),
        ],
        out_specs=pl.BlockSpec((frames, 2 * ROWS, CO, 2 * COLS), lambda f: (f, 0, 0, 0)),
        scratch_shapes=[
            pltpu.VMEM((frames, TALL, HALF, 4 * C), BF16),
            pltpu.VMEM((4, 256, 4 * C), BF16),
            pltpu.VMEM((frames, ROWS, 2, 2 * COLS, 128), F32),
            pltpu.VMEM((frames, ROWS, 2, 2 * COLS, 128), F32),
        ],
        compiler_params=pltpu.CompilerParams(vmem_limit_bytes=60 * 2**20),
        name="upsample",
    )(doubled, w)


def local(
    transformer_latents,
    tile_arrangement,
    entry_conv_weight,
    first_norm_gain,
    first_conv_weight,
    second_norm_gain,
    second_conv_weight,
    temporal_upscale_weight,
    spatial_upscale_weight,
):
    doubled = stem(
        transformer_latents,
        tile_arrangement,
        entry_conv_weight.reshape(27 * LAT, C),
        first_norm_gain,
        first_conv_weight,
        second_norm_gain,
        second_conv_weight,
        temporal_upscale_weight.reshape(3 * C, 2 * C),
    )
    decoded = upsample(
        doubled, jnp.transpose(spatial_upscale_weight, (0, 1, 3, 2)).reshape(9, CO, C)
    )
    return jnp.transpose(decoded, (0, 1, 3, 2))


def solution(mesh):
    return jax.shard_map(
        local,
        mesh=mesh,
        in_specs=(P("seq", "tile", None), P("seq", None), P(), P(), P(), P(), P(), P(), P()),
        out_specs=P("seq", "tile", None, None),
        check_vma=False,
    )
```

```python
import functools

import jax
import jax.numpy as jnp
from jax import lax
from jax.experimental import pallas as pl
from jax.experimental.pallas import tpu as pltpu
from jax.sharding import PartitionSpec as P

EPS = 1e-06
MESH = pl.DeviceIdType.MESH
F32 = jnp.float32
BF16 = jnp.bfloat16

FRAMES = 4
BLOCK = 2
ROWS = 4
COLS = 64
HALF = COLS // 2
LAT = 16
C = 384
CO = 192
BANDS = 16
TALL = ROWS + 2


def silu_norm(v, gain):
    mean = jnp.sum(v * v, axis=-1, keepdims=True) * (1.0 / C)
    w = v * lax.rsqrt(mean + EPS) * gain
    return w + w * jnp.tanh(w)


def before(odd):
    row = lax.broadcasted_iota(jnp.int32, odd.shape, 0)
    return jnp.where(row == 0, 0.0, pltpu.roll(odd, 1, 0))


def after(even):
    row = lax.broadcasted_iota(jnp.int32, even.shape, 0)
    return jnp.where(row == HALF - 1, 0.0, pltpu.roll(even, HALF - 1, 0))


def put_row(ref, t, y, even, odd):
    ref[t, y, 0] = (before(odd) - odd).astype(BF16)
    ref[t, y, 1] = (even + odd).astype(BF16)
    ref[t, y, 2] = (odd - even).astype(BF16)
    ref[t, y, 3] = (even - after(even)).astype(BF16)


def start_weights(w_hbm, u, sems):
    copies = []
    for a in range(3):
        for e, slot in enumerate((0, 1, 3)):
            copies.append(
                pltpu.make_async_copy(
                    w_hbm.at[a, :, e],
                    u.at[slot, :, :, pl.ds((2 - a) * C, C)],
                    sems.at[3 * a + e],
                )
            )
    return copies


def combine_weights(u):
    @pl.loop(0, 3 * (C // 16))
    def _(i):
        b, r = i // (C // 16), 16 * lax.rem(i, C // 16)
        rows = pl.ds(pl.multiple_of(r, 16), 16)
        outer = u[0, b, rows] + u[3, b, rows]
        inner = u[1, b, rows]
        u[1, b, rows] = (outer + inner) * 0.5
        u[2, b, rows] = (outer - inner) * 0.5


def windows(source, t, frames, k, rows):
    return jnp.concatenate(
        [
            jnp.concatenate([source[t + i, y + b, k] for b in range(3)], axis=1)
            for i in range(frames)
            for y in rows
        ],
        axis=0,
    )


def conv(source, u, acc, rows):
    n = HALF * len(rows)
    for k in range(4):
        weight = u[k].reshape(3 * C, 3 * C)
        if len(rows) == 1:
            r = jnp.dot(windows(source, 0, 4, k, rows), weight, preferred_element_type=F32)
            q = [r[n * i : n * (i + 1)] for i in range(4)]
        else:
            r = jnp.dot(windows(source, 0, 2, k, rows), weight, preferred_element_type=F32)
            q = [r[0:n], r[n:]]
            r = jnp.dot(
                windows(source, 2, 2, k, rows), weight[:, 0 : 2 * C], preferred_element_type=F32
            )
            q += [r[0:n], r[n:]]
        for t in range(FRAMES):
            part = q[t][:, 0:C]
            for back in range(1, min(t, 2) + 1):
                part = part + q[t - back][:, back * C : (back + 1) * C]
            if k == 0:
                acc[t, 0, 0:n] = part
            elif k == 1:
                acc[t, 0, 0:n] += part
                acc[t, 1, 0:n] = part
            elif k == 2:
                acc[t, 0, 0:n] += part
                acc[t, 1, 0:n] -= part
            else:
                acc[t, 1, 0:n] -= part


def sum_phases(ws, phase):
    spans = (((0,), (1, 2)), ((0, 1), (2,)))
    for py in range(2):
        for px in range(2):
            for dy in range(2):
                for dx in range(2):
                    total = None
                    for ty in spans[py][dy]:
                        for tx in spans[px][dx]:
                            term = ws[3 * ty + tx].astype(F32)
                            total = term if total is None else total + term
                    at = (2 * dy + dx) * C
                    phase[2 * py + px, 0:CO, at : at + C] = total.astype(BF16)
    phase[:, CO:256] = jnp.zeros((4, 256 - CO, 4 * C), BF16)


def decode_kernel(
    lat_ref,
    arr_ref,
    we_hbm,
    g1_ref,
    w1_hbm,
    g2_ref,
    w2_hbm,
    wt_hbm,
    ws_hbm,
    out_hbm,
    gath,
    lat4,
    late,
    lhs,
    rlo,
    rhi,
    patch,
    mid,
    first,
    h1,
    h2,
    acc,
    s_ref,
    slow_out,
    slow_in,
    fast_out,
    fast_in,
    we,
    u1,
    u2,
    wt,
    ws,
    phase,
    wide,
    low,
    high,
    ready,
    wsem,
    gsend,
    grecv,
    psem,
    hsend,
    hrecv,
    ssend,
    srecv,
    osem,
):
    seq = lax.axis_index("seq")
    band = lax.axis_index("tile")
    half = lax.rem(seq, 2)
    mate = seq + 1 - 2 * half

    odd_band = lax.rem(band, 2)

    loads1 = start_weights(w1_hbm, u1, wsem.at[pl.ds(0, 9)])
    loads2 = start_weights(w2_hbm, u2, wsem.at[pl.ds(9, 9)])
    loads0 = []
    for p in range(9):
        loads0.append(
            pltpu.make_async_copy(
                we_hbm.at[pl.ds(48 * p, 48)], we.at[pl.ds(64 * p, 48)], wsem.at[18 + p]
            )
        )
    load_wt = pltpu.make_async_copy(wt_hbm, wt, wsem.at[27])
    load_ws = pltpu.make_async_copy(ws_hbm, ws, wsem.at[28])

    barrier = pltpu.get_barrier_semaphore()
    for d in range(1, BANDS):
        pl.semaphore_signal(
            barrier, inc=1, device_id=(seq, lax.rem(band + d, BANDS)), device_id_type=MESH
        )
    pl.semaphore_signal(barrier, inc=1, device_id=(mate, band), device_id_type=MESH)
    for load in loads1 + loads0 + [load_ws] + loads2 + [load_wt]:
        load.start()
    pl.semaphore_wait(barrier, BANDS)

    pushes = []
    for d in range(1, BANDS):
        pushes.append(
            pltpu.make_async_remote_copy(
                src_ref=lat_ref,
                dst_ref=gath.at[pl.ds(2 * band, 2)],
                send_sem=gsend.at[d],
                recv_sem=grecv.at[d],
                device_id=(seq, lax.rem(band + d, BANDS)),
                device_id_type=MESH,
            )
        )
    for push in pushes:
        push.start()
    gath[pl.ds(2 * band, 2)] = lat_ref[...]

    for p in range(9):
        we[pl.ds(64 * p + 48, 16)] = jnp.zeros((16, C), BF16)
    we[pl.ds(576, 64)] = jnp.zeros((64, C), BF16)
    rlo[0:2] = jnp.zeros((2, 8, COLS, 128), BF16)
    rhi[0:2] = jnp.zeros((2, 8, COLS, 128), BF16)
    s_ref[0:2] = jnp.zeros((2, TALL, COLS, C), BF16)
    spots = []
    for i in range(BLOCK):
        for o in (-1, 0, 1):
            target = i * BANDS + band + o
            spot = jnp.int32(0)
            for n in range(2 * BANDS):
                spot = jnp.where(arr_ref[0, n] == target, n, spot)
            spots.append(spot)

    for load in loads1:
        load.wait()
    combine_weights(u1)
    load_ws.wait()
    sum_phases(ws, phase)

    for push in pushes:
        push.wait_recv()

    has_up = (band > 0).astype(F32)
    has_down = (band < BANDS - 1).astype(F32)
    picked = []
    for i in range(BLOCK):
        above = gath[spots[3 * i]].astype(F32) * has_up
        own = gath[spots[3 * i + 1]].astype(F32)
        below = gath[spots[3 * i + 2]].astype(F32) * has_down
        picked.append(jnp.concatenate([above[2:4], own, below[0:2]], axis=0))
    lat4[half] = jnp.concatenate(picked, axis=0).astype(BF16)
    swap = pltpu.make_async_remote_copy(
        src_ref=lat4.at[half],
        dst_ref=lat4.at[half],
        send_sem=psem.at[0],
        recv_sem=psem.at[1],
        device_id=(mate, band),
        device_id_type=MESH,
    )
    swap.start()

    place_of = lax.broadcasted_iota(jnp.int32, (16, COLS * LAT), 0)
    column_of = 2 * lax.rem(place_of, 8) + place_of // 8
    spread = (
        lax.rem(lax.broadcasted_iota(jnp.int32, (16, COLS * LAT), 1), 256) // LAT == column_of
    ).astype(F32)
    kk = lax.broadcasted_iota(jnp.int32, (768, 256), 0)
    nn = lax.broadcasted_iota(jnp.int32, (768, 256), 1)
    want = jnp.where(nn < 128, nn, nn - 128 - 64)
    place = (
        (want >= 0)
        & (want < 48)
        & (want // LAT == kk // 256)
        & (lax.rem(want, LAT) == lax.rem(kk, LAT))
    )
    place = place.astype(F32).astype(BF16)

    def relayout(block):
        lat = lat4[block].astype(F32)
        lane = lax.broadcasted_iota(jnp.int32, lat.shape, 1)
        late[0] = jnp.where(lane < LAT, 0.0, pltpu.roll(lat, LAT, 1))
        late[1] = lat
        late[2] = jnp.where(lane >= (COLS - 1) * LAT, 0.0, pltpu.roll(lat, (COLS - 1) * LAT, 1))

        @pl.loop(0, 16)
        def _(r):
            for e in range(3):
                row = late[e, pl.ds(r, 1), :]
                full = (jnp.broadcast_to(row, (16, COLS * LAT)) * spread).astype(BF16)
                for g in range(4):
                    lhs[r, pl.ds(16 * g, 16), 256 * e : 256 * (e + 1)] = full[
                        :, 256 * g : 256 * (g + 1)
                    ]

        @pl.loop(0, 2)
        def _(i):
            r = jnp.dot(
                lhs[pl.ds(8 * i, 8)].reshape(8 * COLS, 768), place, preferred_element_type=F32
            )
            r = jnp.concatenate(
                [
                    r[at : at + 8]
                    for y in range(8)
                    for par in range(2)
                    for at in range(y * COLS + 8 * par, (y + 1) * COLS, 16)
                ],
                axis=0,
            ).astype(BF16)
            t = 2 * block + i
            rlo[t + 2] = r[:, 0:128].reshape(8, COLS, 128)
            rhi[t + 2] = r[:, 128:256].reshape(8, COLS, 128)

    relayout(half)
    for load in loads2:
        load.wait()
    combine_weights(u2)
    swap.wait_recv()
    relayout(1 - half)

    for load in loads0:
        load.wait()

    @pl.loop(0, 4)
    def _(t):
        taps = [(a, b) for a in range(3) for b in range(3)]
        for q in range(5):
            a, b = taps[2 * q]
            v = rlo[t + a, pl.ds(b, TALL)]
            if 2 * q + 1 < 9:
                a, b = taps[2 * q + 1]
                v = v + rhi[t + a, pl.ds(b, TALL)]
            patch[:, 128 * q : 128 * (q + 1)] = v.reshape(TALL * COLS, 128)
        mid[...] = jnp.dot(patch[...], we[...], preferred_element_type=F32)
        for y in range(TALL):
            v = mid[pl.ds(COLS * y, COLS)].astype(BF16)
            if 1 <= y <= ROWS:
                first[t, y - 1] = v
            h = silu_norm(v.astype(F32), 0.5 * g1_ref[...])
            if y == 0:
                h = h * has_up
            if y == TALL - 1:
                h = h * has_down
            put_row(h1, t, y, h[0:HALF], h[HALF:])

    far = lax.rem(band + BANDS - 1 + 2 * odd_band, BANDS)
    near = band + 1 - 2 * odd_band
    far_inside = jnp.where(odd_band == 0, has_up, has_down)
    far_row = 3 * odd_band
    near_row = 3 - far_row
    far_halo = 5 * odd_band
    near_halo = 5 - far_halo
    others = [1 - odd_band + i for i in range(3)]

    def push_to(src, dst, to, send, recv):
        copy = pltpu.make_async_remote_copy(
            src_ref=src,
            dst_ref=dst,
            send_sem=send,
            recv_sem=recv,
            device_id=(seq, to),
            device_id_type=MESH,
        )
        copy.start()
        return copy

    def activate(t, k, y, out=None):
        rows = pl.ds(HALF * k, HALF)
        even = silu_norm(acc[t, 0, rows], 0.5 * g2_ref[...])
        odd = silu_norm(acc[t, 1, rows], 0.5 * g2_ref[...])
        put_row(h2, t, y + 1, even, odd)
        if out is not None:
            out[t, 0:HALF] = even.astype(BF16)
            out[t, HALF:] = odd.astype(BF16)

    conv(h1, u1, acc, [far_row, near_row])
    for t in range(FRAMES):
        activate(t, 0, far_row, slow_out)
    halos = [push_to(slow_out, slow_in, far, hsend.at[0], hrecv.at[0])]
    for t in range(FRAMES):
        activate(t, 1, near_row, fast_out)
    halos.append(push_to(fast_out, fast_in, near, hsend.at[1], hrecv.at[1]))
    conv(h1, u1, acc, [1, 2])
    for t in range(FRAMES):
        activate(t, 0, 1)
        activate(t, 1, 2)

    def finish(t, k, y):
        rows = pl.ds(HALF * k, HALF)
        for par in range(2):
            cols = pl.ds(HALF * par, HALF)
            total = acc[t, par, rows] + first[t, y, cols].astype(F32)
            s_ref[t + 2, y + 1, cols] = total.astype(BF16)

    frames = pl.ds(2, FRAMES)
    halos[1].wait_recv()
    for t in range(FRAMES):
        h = fast_in[t].astype(F32)
        put_row(h2, t, near_halo, h[0:HALF], h[HALF:])
    conv(h2, u2, acc, others)
    for t in range(FRAMES):
        for k in range(3):
            finish(t, k, others[k])
    edges = [
        push_to(
            s_ref.at[frames, near_row + 1],
            s_ref.at[frames, 5 - near_halo],
            near,
            ssend.at[1],
            srecv.at[1],
        )
    ]
    halos[0].wait_recv()
    for t in range(FRAMES):
        h = slow_in[t].astype(F32) * far_inside
        put_row(h2, t, far_halo, h[0:HALF], h[HALF:])
    conv(h2, u2, acc, [far_row])
    for t in range(FRAMES):
        finish(t, 0, far_row)
    edges.append(
        push_to(
            s_ref.at[frames, far_row + 1],
            s_ref.at[frames, 5 - far_halo],
            far,
            ssend.at[0],
            srecv.at[0],
        )
    )

    def double(rows):
        cells = len(rows) * COLS
        stacked = jnp.concatenate(
            [
                jnp.concatenate([s_ref[BLOCK * half + i + a, y] for a in range(3)], axis=1)
                for i in range(BLOCK)
                for y in rows
            ],
            axis=0,
        )
        r = jnp.dot(stacked, wt[...], preferred_element_type=F32)
        for i in range(BLOCK):
            for k, y in enumerate(rows):
                for later in range(2):
                    at = i * cells + k * COLS
                    h = r[at : at + COLS, C * later : C * (later + 1)]
                    even, odd = h[0:HALF], h[HALF:]
                    f = 2 * i + later
                    wide[f, y, :, 0:C] = before(odd).astype(BF16)
                    wide[f, y, :, C : 2 * C] = even.astype(BF16)
                    wide[f, y, :, 2 * C : 3 * C] = odd.astype(BF16)
                    wide[f, y, :, 3 * C : 4 * C] = after(even).astype(BF16)

    outs = []

    def upsample(side, rows):
        py = side + odd_band - 2 * side * odd_band
        at_row = {y: y + odd_band * (3 - 2 * y) for y in rows}
        for px in range(2):
            window = jnp.concatenate(
                [
                    jnp.concatenate(
                        [
                            wide[f, at_row[y] + py + dy, :, C * (px + par) : C * (px + par + 2)]
                            for dy in range(2)
                        ],
                        axis=1,
                    )
                    for f in range(2 * BLOCK)
                    for y in rows
                    for par in range(2)
                ],
                axis=0,
            )
            r = lax.dot_general(
                window,
                phase[2 * py + px],
                (((1,), (1,)), ((), ())),
                preferred_element_type=F32,
            )
            at = 0
            for f in range(2 * BLOCK):
                for y in rows:
                    for par in range(2):
                        cols = pl.ds(2 * par + px, HALF, 4)
                        low[side, f, y, cols, :] = r[at : at + HALF, 0:128]
                        high[side, f, y, cols, :] = r[at : at + HALF, 128:256]
                        at += HALF
        for f in range(2 * BLOCK):
            for y in rows:
                row = 2 * at_row[y] + py
                ready[f, row, 0:128] = low[side, f, y].T.astype(BF16)
                ready[f, row, 128:CO] = high[side, f, y].T[0 : CO - 128].astype(BF16)
                copy = pltpu.make_async_copy(
                    ready.at[f, row], out_hbm.at[f, row], osem.at[len(outs)]
                )
                copy.start()
                outs.append(copy)

    load_wt.wait()
    edges[0].wait_recv()
    double([1, 2, 3, 4, near_halo])
    upsample(1, [0, 1, 2, 3])
    upsample(0, [1, 2, 3])
    edges[1].wait_recv()
    for t in range(FRAMES):
        s_ref[t + 2, far_halo] = (s_ref[t + 2, far_halo].astype(F32) * far_inside).astype(BF16)
    double([far_halo])
    upsample(0, [0])

    for copy in outs:
        copy.wait()
    for push in pushes:
        push.wait_send()
    swap.wait_send()
    for copy in halos + edges:
        copy.wait_send()


def decode(lat, arr, we, g1, w1, g2, w2, wt, ws):
    vmem = pl.BlockSpec(memory_space=pltpu.VMEM)
    smem = pl.BlockSpec(memory_space=pltpu.SMEM)
    hbm = pl.BlockSpec(memory_space=pl.ANY)
    dma = pltpu.SemaphoreType.DMA
    return pl.pallas_call(
        decode_kernel,
        out_shape=jax.ShapeDtypeStruct((2 * BLOCK, 2 * ROWS, CO, 2 * COLS), BF16),
        in_specs=[vmem, smem, hbm, vmem, hbm, vmem, hbm, hbm, hbm],
        out_specs=hbm,
        scratch_shapes=[
            pltpu.VMEM((2 * BANDS, ROWS, COLS * LAT), BF16),
            pltpu.VMEM((2, 16, COLS * LAT), BF16),
            pltpu.VMEM((3, 16, COLS * LAT), F32),
            pltpu.VMEM((16, COLS, 768), BF16),
            pltpu.VMEM((6, 8, COLS, 128), BF16),
            pltpu.VMEM((6, 8, COLS, 128), BF16),
            pltpu.VMEM((TALL * COLS, 640), BF16),
            pltpu.VMEM((TALL * COLS, C), F32),
            pltpu.VMEM((FRAMES, ROWS, COLS, C), BF16),
            pltpu.VMEM((FRAMES, TALL, 4, HALF, C), BF16),
            pltpu.VMEM((FRAMES, TALL, 4, HALF, C), BF16),
            pltpu.VMEM((FRAMES, 2, 3 * HALF, C), F32),
            pltpu.VMEM((FRAMES + 2, TALL, COLS, C), BF16),
            pltpu.VMEM((FRAMES, COLS, C), BF16),
            pltpu.VMEM((FRAMES, COLS, C), BF16),
            pltpu.VMEM((FRAMES, COLS, C), BF16),
            pltpu.VMEM((FRAMES, COLS, C), BF16),
            pltpu.VMEM((640, C), BF16),
            pltpu.VMEM((4, 3, C, 3 * C), BF16),
            pltpu.VMEM((4, 3, C, 3 * C), BF16),
            pltpu.VMEM((3 * C, 2 * C), BF16),
            pltpu.VMEM((9, CO, C), BF16),
            pltpu.VMEM((4, 256, 4 * C), BF16),
            pltpu.VMEM((2 * BLOCK, TALL, HALF, 4 * C), BF16),
            pltpu.VMEM((2, 2 * BLOCK, ROWS, 2 * COLS, 128), F32),
            pltpu.VMEM((2, 2 * BLOCK, ROWS, 2 * COLS, 128), F32),
            pltpu.VMEM((2 * BLOCK, 2 * ROWS, CO, 2 * COLS), BF16),
            dma((29,)),
            dma((BANDS,)),
            dma((BANDS,)),
            dma((2,)),
            dma((2,)),
            dma((2,)),
            dma((2,)),
            dma((2,)),
            dma((4 * BLOCK * ROWS,)),
        ],
        compiler_params=pltpu.CompilerParams(
            collective_id=0, has_side_effects=True, vmem_limit_bytes=60 * 2**20
        ),
        name="decode",
    )(lat, arr, we, g1, w1, g2, w2, wt, ws)


def local(
    transformer_latents,
    tile_arrangement,
    entry_conv_weight,
    first_norm_gain,
    first_conv_weight,
    second_norm_gain,
    second_conv_weight,
    temporal_upscale_weight,
    spatial_upscale_weight,
):
    decoded = decode(
        transformer_latents,
        tile_arrangement,
        entry_conv_weight.reshape(27 * LAT, C),
        first_norm_gain,
        first_conv_weight,
        second_norm_gain,
        second_conv_weight,
        temporal_upscale_weight.reshape(3 * C, 2 * C),
        jnp.transpose(spatial_upscale_weight, (0, 1, 3, 2)).reshape(9, CO, C),
    )
    return jnp.transpose(decoded, (0, 1, 3, 2))


def solution(mesh):
    return jax.shard_map(
        local,
        mesh=mesh,
        in_specs=(P("seq", "tile", None), P("seq", None), P(), P(), P(), P(), P(), P(), P()),
        out_specs=P("seq", "tile", None, None),
        check_vma=False,
    )
```

```python
import functools

import jax
import jax.numpy as jnp
from jax import lax
from jax.experimental import pallas as pl
from jax.experimental.pallas import tpu as pltpu
from jax.sharding import PartitionSpec as P

EPS = 1e-06
MESH = pl.DeviceIdType.MESH
F32 = jnp.float32
BF16 = jnp.bfloat16

FRAMES = 4
BLOCK = 2
ROWS = 4
COLS = 64
HALF = COLS // 2
LAT = 16
C = 384
CO = 192
BANDS = 16
TALL = ROWS + 2


def silu_norm(v, gain):
    mean = jnp.sum(v * v, axis=-1, keepdims=True) * (1.0 / C)
    w = v * lax.rsqrt(mean + EPS) * gain
    return w + w * jnp.tanh(w)


def before(odd):
    row = lax.broadcasted_iota(jnp.int32, odd.shape, 0)
    return jnp.where(row == 0, 0.0, pltpu.roll(odd, 1, 0))


def after(even):
    row = lax.broadcasted_iota(jnp.int32, even.shape, 0)
    return jnp.where(row == HALF - 1, 0.0, pltpu.roll(even, HALF - 1, 0))


def put_row(ref, t, y, even, odd):
    ref[t, y, 0] = (before(odd) - odd).astype(BF16)
    ref[t, y, 1] = (even + odd).astype(BF16)
    ref[t, y, 2] = (odd - even).astype(BF16)
    ref[t, y, 3] = (even - after(even)).astype(BF16)


def start_weights(w_hbm, u, sems):
    copies = []
    for a in range(3):
        for e, slot in enumerate((0, 1, 3)):
            copies.append(
                pltpu.make_async_copy(
                    w_hbm.at[a, :, e],
                    u.at[slot, :, :, pl.ds((2 - a) * C, C)],
                    sems.at[3 * a + e],
                )
            )
    return copies


def combine_weights(u):
    @pl.loop(0, 3 * (C // 16))
    def _(i):
        b, r = i // (C // 16), 16 * lax.rem(i, C // 16)
        rows = pl.ds(pl.multiple_of(r, 16), 16)
        outer = u[0, b, rows] + u[3, b, rows]
        inner = u[1, b, rows]
        u[1, b, rows] = (outer + inner) * 0.5
        u[2, b, rows] = (outer - inner) * 0.5


def windows(source, t, frames, k, rows):
    return jnp.concatenate(
        [
            jnp.concatenate([source[t + i, y + b, k] for b in range(3)], axis=1)
            for i in range(frames)
            for y in rows
        ],
        axis=0,
    )


def conv(source, u, acc, rows):
    n = HALF * len(rows)
    for k in range(4):
        weight = u[k].reshape(3 * C, 3 * C)
        if len(rows) == 1:
            r = jnp.dot(windows(source, 0, 4, k, rows), weight, preferred_element_type=F32)
            q = [r[n * i : n * (i + 1)] for i in range(4)]
        else:
            r = jnp.dot(windows(source, 0, 2, k, rows), weight, preferred_element_type=F32)
            q = [r[0:n], r[n:]]
            r = jnp.dot(
                windows(source, 2, 2, k, rows), weight[:, 0 : 2 * C], preferred_element_type=F32
            )
            q += [r[0:n], r[n:]]
        for t in range(FRAMES):
            part = q[t][:, 0:C]
            for back in range(1, min(t, 2) + 1):
                part = part + q[t - back][:, back * C : (back + 1) * C]
            if k == 0:
                acc[t, 0, 0:n] = part
            elif k == 1:
                acc[t, 0, 0:n] += part
                acc[t, 1, 0:n] = part
            elif k == 2:
                acc[t, 0, 0:n] += part
                acc[t, 1, 0:n] -= part
            else:
                acc[t, 1, 0:n] -= part


def sum_phases(ws, phase):
    spans = (((0,), (1, 2)), ((0, 1), (2,)))
    for py in range(2):
        for px in range(2):
            for dy in range(2):
                for dx in range(2):
                    total = None
                    for ty in spans[py][dy]:
                        for tx in spans[px][dx]:
                            term = ws[3 * ty + tx].astype(F32)
                            total = term if total is None else total + term
                    at = (2 * dy + dx) * C
                    phase[2 * py + px, 0:CO, at : at + C] = total.astype(BF16)
    phase[:, CO:256] = jnp.zeros((4, 256 - CO, 4 * C), BF16)


def decode_kernel(
    lat_ref,
    arr_ref,
    we_hbm,
    g1_ref,
    w1_hbm,
    g2_ref,
    w2_hbm,
    wt_hbm,
    ws_hbm,
    out_hbm,
    gath,
    lat4,
    late,
    lhs,
    rlo,
    rhi,
    patch,
    mid,
    first,
    h1,
    h2,
    acc,
    s_ref,
    slow_out,
    slow_in,
    fast_out,
    fast_in,
    we,
    u1,
    u2,
    wt,
    ws,
    phase,
    wide,
    low,
    high,
    ready,
    wsem,
    gsend,
    grecv,
    psem,
    hsend,
    hrecv,
    ssend,
    srecv,
    osem,
):
    seq = lax.axis_index("seq")
    band = lax.axis_index("tile")
    half = lax.rem(seq, 2)
    mate = seq + 1 - 2 * half

    odd_band = lax.rem(band, 2)

    loads1 = start_weights(w1_hbm, u1, wsem.at[pl.ds(0, 9)])
    loads2 = start_weights(w2_hbm, u2, wsem.at[pl.ds(9, 9)])
    loads0 = []
    for p in range(9):
        loads0.append(
            pltpu.make_async_copy(
                we_hbm.at[pl.ds(48 * p, 48)], we.at[pl.ds(64 * p, 48)], wsem.at[18 + p]
            )
        )
    load_wt = pltpu.make_async_copy(wt_hbm, wt, wsem.at[27])
    load_ws = pltpu.make_async_copy(ws_hbm, ws, wsem.at[28])

    barrier = pltpu.get_barrier_semaphore()
    for d in range(1, BANDS):
        pl.semaphore_signal(
            barrier, inc=1, device_id=(seq, lax.rem(band + d, BANDS)), device_id_type=MESH
        )
    pl.semaphore_signal(barrier, inc=1, device_id=(mate, band), device_id_type=MESH)
    for load in loads1 + loads0 + [load_ws] + loads2 + [load_wt]:
        load.start()
    pl.semaphore_wait(barrier, BANDS)

    pushes = []
    for d in range(1, BANDS):
        pushes.append(
            pltpu.make_async_remote_copy(
                src_ref=lat_ref,
                dst_ref=gath.at[pl.ds(2 * band, 2)],
                send_sem=gsend.at[d],
                recv_sem=grecv.at[d],
                device_id=(seq, lax.rem(band + d, BANDS)),
                device_id_type=MESH,
            )
        )
    for push in pushes:
        push.start()
    gath[pl.ds(2 * band, 2)] = lat_ref[...]

    for p in range(9):
        we[pl.ds(64 * p + 48, 16)] = jnp.zeros((16, C), BF16)
    we[pl.ds(576, 64)] = jnp.zeros((64, C), BF16)
    rlo[0:2] = jnp.zeros((2, 8, COLS, 128), BF16)
    rhi[0:2] = jnp.zeros((2, 8, COLS, 128), BF16)
    s_ref[0:2] = jnp.zeros((2, TALL, COLS, C), BF16)
    spots = []
    for i in range(BLOCK):
        for o in (-1, 0, 1):
            target = i * BANDS + band + o
            spot = jnp.int32(0)
            for n in range(2 * BANDS):
                spot = jnp.where(arr_ref[0, n] == target, n, spot)
            spots.append(spot)

    for load in loads1:
        load.wait()
    combine_weights(u1)
    load_ws.wait()
    sum_phases(ws, phase)

    for push in pushes:
        push.wait_recv()

    has_up = (band > 0).astype(F32)
    has_down = (band < BANDS - 1).astype(F32)
    picked = []
    for i in range(BLOCK):
        above = gath[spots[3 * i]].astype(F32) * has_up
        own = gath[spots[3 * i + 1]].astype(F32)
        below = gath[spots[3 * i + 2]].astype(F32) * has_down
        picked.append(jnp.concatenate([above[2:4], own, below[0:2]], axis=0))
    lat4[half] = jnp.concatenate(picked, axis=0).astype(BF16)
    swap = pltpu.make_async_remote_copy(
        src_ref=lat4.at[half],
        dst_ref=lat4.at[half],
        send_sem=psem.at[0],
        recv_sem=psem.at[1],
        device_id=(mate, band),
        device_id_type=MESH,
    )
    swap.start()

    place_of = lax.broadcasted_iota(jnp.int32, (16, COLS * LAT), 0)
    column_of = 2 * lax.rem(place_of, 8) + place_of // 8
    spread = (
        lax.rem(lax.broadcasted_iota(jnp.int32, (16, COLS * LAT), 1), 256) // LAT == column_of
    ).astype(F32)
    kk = lax.broadcasted_iota(jnp.int32, (256, 128), 0)
    nn = lax.broadcasted_iota(jnp.int32, (256, 128), 1)
    place = (lax.rem(nn, LAT) == lax.rem(kk, LAT)).astype(F32).astype(BF16)
    lane = lax.broadcasted_iota(jnp.int32, (HALF, 128), 1)
    slot = lane // LAT

    def taps(left, centre, right, base):
        picked = jnp.where(slot == base + 1, centre, 0.0)
        picked = jnp.where(slot == base, left, picked)
        return jnp.where(slot == base + 2, right, picked).astype(BF16)

    def relayout(block):
        late[...] = lat4[block].astype(F32)

        @pl.loop(0, 16)
        def _(r):
            row = late[pl.ds(r, 1), :]
            full = (jnp.broadcast_to(row, (16, COLS * LAT)) * spread).astype(BF16)
            for g in range(4):
                lhs[r, pl.ds(16 * g, 16)] = full[:, 256 * g : 256 * (g + 1)]

        for i in range(2):
            r = jnp.dot(
                lhs[pl.ds(8 * i, 8)].reshape(8 * COLS, 256), place, preferred_element_type=F32
            )
            t = 2 * block + i
            for y in range(8):
                even, odd = (
                    jnp.concatenate(
                        [r[at : at + 8] for at in range(y * COLS + 8 * par, (y + 1) * COLS, 16)],
                        axis=0,
                    )
                    for par in range(2)
                )
                left, right = before(odd), after(even)
                for ref, base in ((rlo, 0), (rhi, 4)):
                    ref[t + 2, y, 0:HALF] = taps(left, even, odd, base)
                    ref[t + 2, y, HALF:] = taps(even, odd, right, base)

    relayout(half)
    for load in loads2:
        load.wait()
    combine_weights(u2)
    swap.wait_recv()
    relayout(1 - half)

    for load in loads0:
        load.wait()

    @pl.loop(0, 4)
    def _(t):
        taps = [(a, b) for a in range(3) for b in range(3)]
        for q in range(5):
            a, b = taps[2 * q]
            v = rlo[t + a, pl.ds(b, TALL)]
            if 2 * q + 1 < 9:
                a, b = taps[2 * q + 1]
                v = v + rhi[t + a, pl.ds(b, TALL)]
            patch[:, 128 * q : 128 * (q + 1)] = v.reshape(TALL * COLS, 128)
        mid[...] = jnp.dot(patch[...], we[...], preferred_element_type=F32)
        for y in range(TALL):
            v = mid[pl.ds(COLS * y, COLS)].astype(BF16)
            if 1 <= y <= ROWS:
                first[t, y - 1] = v
            h = silu_norm(v.astype(F32), 0.5 * g1_ref[...])
            if y == 0:
                h = h * has_up
            if y == TALL - 1:
                h = h * has_down
            put_row(h1, t, y, h[0:HALF], h[HALF:])

    far = lax.rem(band + BANDS - 1 + 2 * odd_band, BANDS)
    near = band + 1 - 2 * odd_band
    far_inside = jnp.where(odd_band == 0, has_up, has_down)
    far_row = 3 * odd_band
    near_row = 3 - far_row
    far_halo = 5 * odd_band
    near_halo = 5 - far_halo
    others = [1 - odd_band + i for i in range(3)]

    def push_to(src, dst, to, send, recv):
        copy = pltpu.make_async_remote_copy(
            src_ref=src,
            dst_ref=dst,
            send_sem=send,
            recv_sem=recv,
            device_id=(seq, to),
            device_id_type=MESH,
        )
        copy.start()
        return copy

    def activate(t, k, y, out=None):
        rows = pl.ds(HALF * k, HALF)
        even = silu_norm(acc[t, 0, rows], 0.5 * g2_ref[...])
        odd = silu_norm(acc[t, 1, rows], 0.5 * g2_ref[...])
        put_row(h2, t, y + 1, even, odd)
        if out is not None:
            out[t, 0:HALF] = even.astype(BF16)
            out[t, HALF:] = odd.astype(BF16)

    conv(h1, u1, acc, [far_row, near_row])
    for t in range(FRAMES):
        activate(t, 0, far_row, slow_out)
    halos = [push_to(slow_out, slow_in, far, hsend.at[0], hrecv.at[0])]
    for t in range(FRAMES):
        activate(t, 1, near_row, fast_out)
    halos.append(push_to(fast_out, fast_in, near, hsend.at[1], hrecv.at[1]))
    conv(h1, u1, acc, [1, 2])
    for t in range(FRAMES):
        activate(t, 0, 1)
        activate(t, 1, 2)

    def finish(t, k, y):
        rows = pl.ds(HALF * k, HALF)
        for par in range(2):
            cols = pl.ds(HALF * par, HALF)
            total = acc[t, par, rows] + first[t, y, cols].astype(F32)
            s_ref[t + 2, y + 1, cols] = total.astype(BF16)

    frames = pl.ds(2, FRAMES)
    halos[1].wait_recv()
    for t in range(FRAMES):
        h = fast_in[t].astype(F32)
        put_row(h2, t, near_halo, h[0:HALF], h[HALF:])
    conv(h2, u2, acc, others)
    for t in range(FRAMES):
        for k in range(3):
            finish(t, k, others[k])
    edges = [
        push_to(
            s_ref.at[frames, near_row + 1],
            s_ref.at[frames, 5 - near_halo],
            near,
            ssend.at[1],
            srecv.at[1],
        )
    ]
    halos[0].wait_recv()
    for t in range(FRAMES):
        h = slow_in[t].astype(F32) * far_inside
        put_row(h2, t, far_halo, h[0:HALF], h[HALF:])
    conv(h2, u2, acc, [far_row])
    for t in range(FRAMES):
        finish(t, 0, far_row)
    edges.append(
        push_to(
            s_ref.at[frames, far_row + 1],
            s_ref.at[frames, 5 - far_halo],
            far,
            ssend.at[0],
            srecv.at[0],
        )
    )

    def double(rows):
        cells = len(rows) * COLS
        stacked = jnp.concatenate(
            [
                jnp.concatenate([s_ref[BLOCK * half + i + a, y] for a in range(3)], axis=1)
                for i in range(BLOCK)
                for y in rows
            ],
            axis=0,
        )
        r = jnp.dot(stacked, wt[...], preferred_element_type=F32)
        for i in range(BLOCK):
            for k, y in enumerate(rows):
                for later in range(2):
                    at = i * cells + k * COLS
                    h = r[at : at + COLS, C * later : C * (later + 1)]
                    even, odd = h[0:HALF], h[HALF:]
                    f = 2 * i + later
                    wide[f, y, :, 0:C] = before(odd).astype(BF16)
                    wide[f, y, :, C : 2 * C] = even.astype(BF16)
                    wide[f, y, :, 2 * C : 3 * C] = odd.astype(BF16)
                    wide[f, y, :, 3 * C : 4 * C] = after(even).astype(BF16)

    outs = []

    def upsample(side, rows):
        py = side + odd_band - 2 * side * odd_band
        at_row = {y: y + odd_band * (3 - 2 * y) for y in rows}
        for px in range(2):
            window = jnp.concatenate(
                [
                    jnp.concatenate(
                        [
                            wide[f, at_row[y] + py + dy, :, C * (px + par) : C * (px + par + 2)]
                            for dy in range(2)
                        ],
                        axis=1,
                    )
                    for f in range(2 * BLOCK)
                    for y in rows
                    for par in range(2)
                ],
                axis=0,
            )
            r = lax.dot_general(
                window,
                phase[2 * py + px],
                (((1,), (1,)), ((), ())),
                preferred_element_type=F32,
            )
            at = 0
            for f in range(2 * BLOCK):
                for y in rows:
                    for par in range(2):
                        cols = pl.ds(2 * par + px, HALF, 4)
                        low[side, f, y, cols, :] = r[at : at + HALF, 0:128]
                        high[side, f, y, cols, :] = r[at : at + HALF, 128:256]
                        at += HALF
        for f in range(2 * BLOCK):
            for y in rows:
                row = 2 * at_row[y] + py
                ready[f, row, 0:128] = low[side, f, y].T.astype(BF16)
                ready[f, row, 128:CO] = high[side, f, y].T[0 : CO - 128].astype(BF16)
                copy = pltpu.make_async_copy(
                    ready.at[f, row], out_hbm.at[f, row], osem.at[len(outs)]
                )
                copy.start()
                outs.append(copy)

    load_wt.wait()
    edges[0].wait_recv()
    double([1, 2, 3, 4, near_halo])
    upsample(1, [0, 1, 2, 3])
    upsample(0, [1, 2, 3])
    edges[1].wait_recv()
    for t in range(FRAMES):
        s_ref[t + 2, far_halo] = (s_ref[t + 2, far_halo].astype(F32) * far_inside).astype(BF16)
    double([far_halo])
    upsample(0, [0])

    for copy in outs:
        copy.wait()
    for push in pushes:
        push.wait_send()
    swap.wait_send()
    for copy in halos + edges:
        copy.wait_send()


def decode(lat, arr, we, g1, w1, g2, w2, wt, ws):
    vmem = pl.BlockSpec(memory_space=pltpu.VMEM)
    smem = pl.BlockSpec(memory_space=pltpu.SMEM)
    hbm = pl.BlockSpec(memory_space=pl.ANY)
    dma = pltpu.SemaphoreType.DMA
    return pl.pallas_call(
        decode_kernel,
        out_shape=jax.ShapeDtypeStruct((2 * BLOCK, 2 * ROWS, CO, 2 * COLS), BF16),
        in_specs=[vmem, smem, hbm, vmem, hbm, vmem, hbm, hbm, hbm],
        out_specs=hbm,
        scratch_shapes=[
            pltpu.VMEM((2 * BANDS, ROWS, COLS * LAT), BF16),
            pltpu.VMEM((2, 16, COLS * LAT), BF16),
            pltpu.VMEM((16, COLS * LAT), F32),
            pltpu.VMEM((16, COLS, 256), BF16),
            pltpu.VMEM((6, 8, COLS, 128), BF16),
            pltpu.VMEM((6, 8, COLS, 128), BF16),
            pltpu.VMEM((TALL * COLS, 640), BF16),
            pltpu.VMEM((TALL * COLS, C), F32),
            pltpu.VMEM((FRAMES, ROWS, COLS, C), BF16),
            pltpu.VMEM((FRAMES, TALL, 4, HALF, C), BF16),
            pltpu.VMEM((FRAMES, TALL, 4, HALF, C), BF16),
            pltpu.VMEM((FRAMES, 2, 3 * HALF, C), F32),
            pltpu.VMEM((FRAMES + 2, TALL, COLS, C), BF16),
            pltpu.VMEM((FRAMES, COLS, C), BF16),
            pltpu.VMEM((FRAMES, COLS, C), BF16),
            pltpu.VMEM((FRAMES, COLS, C), BF16),
            pltpu.VMEM((FRAMES, COLS, C), BF16),
            pltpu.VMEM((640, C), BF16),
            pltpu.VMEM((4, 3, C, 3 * C), BF16),
            pltpu.VMEM((4, 3, C, 3 * C), BF16),
            pltpu.VMEM((3 * C, 2 * C), BF16),
            pltpu.VMEM((9, CO, C), BF16),
            pltpu.VMEM((4, 256, 4 * C), BF16),
            pltpu.VMEM((2 * BLOCK, TALL, HALF, 4 * C), BF16),
            pltpu.VMEM((2, 2 * BLOCK, ROWS, 2 * COLS, 128), F32),
            pltpu.VMEM((2, 2 * BLOCK, ROWS, 2 * COLS, 128), F32),
            pltpu.VMEM((2 * BLOCK, 2 * ROWS, CO, 2 * COLS), BF16),
            dma((29,)),
            dma((BANDS,)),
            dma((BANDS,)),
            dma((2,)),
            dma((2,)),
            dma((2,)),
            dma((2,)),
            dma((2,)),
            dma((4 * BLOCK * ROWS,)),
        ],
        compiler_params=pltpu.CompilerParams(
            collective_id=0, has_side_effects=True, vmem_limit_bytes=60 * 2**20
        ),
        name="decode",
    )(lat, arr, we, g1, w1, g2, w2, wt, ws)


def hand_over_kernel(src, dst, sems):
    copies = []
    for f in range(2 * BLOCK):
        for part in range(4):
            rows = pl.ds(2 * part, 2)
            copies.append(
                pltpu.make_async_copy(src.at[f, rows], dst.at[f, rows], sems.at[4 * f + part])
            )
    for copy in copies:
        copy.start()
    for copy in copies:
        copy.wait()


def hand_over(decoded):
    return pl.pallas_call(
        hand_over_kernel,
        out_shape=jax.ShapeDtypeStruct(decoded.shape, decoded.dtype),
        in_specs=[pl.BlockSpec(memory_space=pl.ANY)],
        out_specs=pl.BlockSpec(memory_space=pl.ANY),
        scratch_shapes=[pltpu.SemaphoreType.DMA((8 * BLOCK,))],
        compiler_params=pltpu.CompilerParams(vmem_limit_bytes=63 * 2**20),
        name="hand_over",
    )(decoded)


def local(
    transformer_latents,
    tile_arrangement,
    entry_conv_weight,
    first_norm_gain,
    first_conv_weight,
    second_norm_gain,
    second_conv_weight,
    temporal_upscale_weight,
    spatial_upscale_weight,
):
    decoded = decode(
        transformer_latents,
        tile_arrangement,
        entry_conv_weight.reshape(27 * LAT, C),
        first_norm_gain,
        first_conv_weight,
        second_norm_gain,
        second_conv_weight,
        temporal_upscale_weight.reshape(3 * C, 2 * C),
        jnp.transpose(spatial_upscale_weight, (0, 1, 3, 2)).reshape(9, CO, C),
    )
    return jnp.transpose(hand_over(decoded), (0, 1, 3, 2))


def solution(mesh):
    return jax.shard_map(
        local,
        mesh=mesh,
        in_specs=(P("seq", "tile", None), P("seq", None), P(), P(), P(), P(), P(), P(), P()),
        out_specs=P("seq", "tile", None, None),
        check_vma=False,
    )
```

```python
import functools

import jax
import jax.numpy as jnp
from jax import lax
from jax.experimental import pallas as pl
from jax.experimental.pallas import tpu as pltpu
from jax.sharding import PartitionSpec as P

EPS = 1e-06
MESH = pl.DeviceIdType.MESH
F32 = jnp.float32
BF16 = jnp.bfloat16

FRAMES = 4
BLOCK = 2
ROWS = 4
COLS = 64
HALF = COLS // 2
LAT = 16
C = 384
CO = 192
BANDS = 16
TALL = ROWS + 2


def silu_norm(v, gain):
    mean = jnp.sum(v * v, axis=-1, keepdims=True) * (1.0 / C)
    w = v * lax.rsqrt(mean + EPS) * gain
    return w + w * jnp.tanh(w)


def before(odd):
    row = lax.broadcasted_iota(jnp.int32, odd.shape, 0)
    return jnp.where(row == 0, 0.0, pltpu.roll(odd, 1, 0))


def after(even):
    row = lax.broadcasted_iota(jnp.int32, even.shape, 0)
    return jnp.where(row == HALF - 1, 0.0, pltpu.roll(even, HALF - 1, 0))


def put_row(ref, t, y, even, odd):
    ref[t, y, 0] = (before(odd) - odd).astype(BF16)
    ref[t, y, 1] = (even + odd).astype(BF16)
    ref[t, y, 2] = (odd - even).astype(BF16)
    ref[t, y, 3] = (even - after(even)).astype(BF16)


def start_weights(w_hbm, u, sems):
    copies = []
    for a in range(3):
        for e, slot in enumerate((0, 1, 3)):
            copies.append(
                pltpu.make_async_copy(
                    w_hbm.at[a, :, e],
                    u.at[slot, :, :, pl.ds((2 - a) * C, C)],
                    sems.at[3 * a + e],
                )
            )
    return copies


def combine_weights(u):
    @pl.loop(0, 3 * (C // 16))
    def _(i):
        b, r = i // (C // 16), 16 * lax.rem(i, C // 16)
        rows = pl.ds(pl.multiple_of(r, 16), 16)
        outer = u[0, b, rows] + u[3, b, rows]
        inner = u[1, b, rows]
        u[1, b, rows] = (outer + inner) * 0.5
        u[2, b, rows] = (outer - inner) * 0.5


def windows(source, t, frames, k, rows):
    return jnp.concatenate(
        [
            jnp.concatenate([source[t + i, y + b, k] for b in range(3)], axis=1)
            for i in range(frames)
            for y in rows
        ],
        axis=0,
    )


def conv(source, u, acc, rows):
    n = HALF * len(rows)
    for k in range(4):
        weight = u[k].reshape(3 * C, 3 * C)
        if len(rows) == 1:
            r = jnp.dot(windows(source, 0, 4, k, rows), weight, preferred_element_type=F32)
            q = [r[n * i : n * (i + 1)] for i in range(4)]
        else:
            r = jnp.dot(windows(source, 0, 2, k, rows), weight, preferred_element_type=F32)
            q = [r[0:n], r[n:]]
            r = jnp.dot(
                windows(source, 2, 2, k, rows), weight[:, 0 : 2 * C], preferred_element_type=F32
            )
            q += [r[0:n], r[n:]]
        for t in range(FRAMES):
            part = q[t][:, 0:C]
            for back in range(1, min(t, 2) + 1):
                part = part + q[t - back][:, back * C : (back + 1) * C]
            if k == 0:
                acc[t, 0, 0:n] = part
            elif k == 1:
                acc[t, 0, 0:n] += part
                acc[t, 1, 0:n] = part
            elif k == 2:
                acc[t, 0, 0:n] += part
                acc[t, 1, 0:n] -= part
            else:
                acc[t, 1, 0:n] -= part


def sum_phases(ws, phase):
    spans = (((0,), (1, 2)), ((0, 1), (2,)))
    for py in range(2):
        for px in range(2):
            for dy in range(2):
                for dx in range(2):
                    total = None
                    for ty in spans[py][dy]:
                        for tx in spans[px][dx]:
                            term = ws[3 * ty + tx].astype(F32)
                            total = term if total is None else total + term
                    at = (2 * dy + dx) * C
                    phase[2 * py + px, 0:CO, at : at + C] = total.astype(BF16)
    phase[:, CO:256] = jnp.zeros((4, 256 - CO, 4 * C), BF16)


def decode_kernel(
    lat_hbm,
    arr_hbm,
    we_hbm,
    g1_hbm,
    w1_hbm,
    g2_hbm,
    w2_hbm,
    wt_hbm,
    ws_hbm,
    out_ref,
    arr_ref,
    g1_ref,
    g2_ref,
    gath,
    lat4,
    late,
    lhs,
    rlo,
    rhi,
    patch,
    mid,
    first,
    h1,
    h2,
    acc,
    s_ref,
    slow_out,
    slow_in,
    fast_out,
    fast_in,
    we,
    u1,
    u2,
    wt,
    ws,
    phase,
    wide,
    low,
    high,
    wsem,
    gsend,
    grecv,
    psem,
    hsend,
    hrecv,
    ssend,
    srecv,
):
    seq = lax.axis_index("seq")
    band = lax.axis_index("tile")
    half = lax.rem(seq, 2)
    mate = seq + 1 - 2 * half

    odd_band = lax.rem(band, 2)

    loads1 = start_weights(w1_hbm, u1, wsem.at[pl.ds(0, 9)])
    loads2 = start_weights(w2_hbm, u2, wsem.at[pl.ds(9, 9)])
    loads0 = []
    for p in range(9):
        loads0.append(
            pltpu.make_async_copy(
                we_hbm.at[pl.ds(48 * p, 48)], we.at[pl.ds(64 * p, 48)], wsem.at[18 + p]
            )
        )
    load_wt = pltpu.make_async_copy(wt_hbm, wt, wsem.at[27])
    load_arr = pltpu.make_async_copy(arr_hbm, arr_ref, wsem.at[32])
    load_gains = [
        pltpu.make_async_copy(g1_hbm, g1_ref, wsem.at[30]),
        pltpu.make_async_copy(g2_hbm, g2_ref, wsem.at[31]),
    ]
    load_ws = pltpu.make_async_copy(ws_hbm, ws, wsem.at[28])

    barrier = pltpu.get_barrier_semaphore()
    for d in range(1, BANDS):
        pl.semaphore_signal(
            barrier, inc=1, device_id=(seq, lax.rem(band + d, BANDS)), device_id_type=MESH
        )
    pl.semaphore_signal(barrier, inc=1, device_id=(mate, band), device_id_type=MESH)
    for load in [load_arr] + load_gains + loads1 + loads0 + [load_ws] + loads2 + [load_wt]:
        load.start()
    pl.semaphore_wait(barrier, BANDS)

    pushes = []
    for d in range(1, BANDS):
        pushes.append(
            pltpu.make_async_remote_copy(
                src_ref=lat_hbm,
                dst_ref=gath.at[pl.ds(2 * band, 2)],
                send_sem=gsend.at[d],
                recv_sem=grecv.at[d],
                device_id=(seq, lax.rem(band + d, BANDS)),
                device_id_type=MESH,
            )
        )
    for push in pushes:
        push.start()
    load_own = pltpu.make_async_copy(lat_hbm, gath.at[pl.ds(2 * band, 2)], wsem.at[29])
    load_own.start()
    load_own.wait()

    for p in range(9):
        we[pl.ds(64 * p + 48, 16)] = jnp.zeros((16, C), BF16)
    we[pl.ds(576, 64)] = jnp.zeros((64, C), BF16)
    rlo[0:2] = jnp.zeros((2, 8, COLS, 128), BF16)
    rhi[0:2] = jnp.zeros((2, 8, COLS, 128), BF16)
    s_ref[0:2] = jnp.zeros((2, TALL, COLS, C), BF16)
    load_arr.wait()
    spots = []
    for i in range(BLOCK):
        for o in (-1, 0, 1):
            target = i * BANDS + band + o
            spot = jnp.int32(0)
            for n in range(2 * BANDS):
                spot = jnp.where(arr_ref[0, n] == target, n, spot)
            spots.append(spot)

    for load in loads1:
        load.wait()
    combine_weights(u1)
    load_ws.wait()
    sum_phases(ws, phase)

    for push in pushes:
        push.wait_recv()

    has_up = (band > 0).astype(F32)
    has_down = (band < BANDS - 1).astype(F32)
    picked = []
    for i in range(BLOCK):
        above = gath[spots[3 * i]].astype(F32) * has_up
        own = gath[spots[3 * i + 1]].astype(F32)
        below = gath[spots[3 * i + 2]].astype(F32) * has_down
        picked.append(jnp.concatenate([above[2:4], own, below[0:2]], axis=0))
    lat4[half] = jnp.concatenate(picked, axis=0).astype(BF16)
    swap = pltpu.make_async_remote_copy(
        src_ref=lat4.at[half],
        dst_ref=lat4.at[half],
        send_sem=psem.at[0],
        recv_sem=psem.at[1],
        device_id=(mate, band),
        device_id_type=MESH,
    )
    swap.start()

    place_of = lax.broadcasted_iota(jnp.int32, (16, COLS * LAT), 0)
    column_of = 2 * lax.rem(place_of, 8) + place_of // 8
    spread = (
        lax.rem(lax.broadcasted_iota(jnp.int32, (16, COLS * LAT), 1), 256) // LAT == column_of
    ).astype(F32)
    kk = lax.broadcasted_iota(jnp.int32, (256, 128), 0)
    nn = lax.broadcasted_iota(jnp.int32, (256, 128), 1)
    place = (lax.rem(nn, LAT) == lax.rem(kk, LAT)).astype(F32).astype(BF16)
    lane = lax.broadcasted_iota(jnp.int32, (HALF, 128), 1)
    slot = lane // LAT

    def taps(left, centre, right, base):
        picked = jnp.where(slot == base + 1, centre, 0.0)
        picked = jnp.where(slot == base, left, picked)
        return jnp.where(slot == base + 2, right, picked).astype(BF16)

    def relayout(block):
        late[...] = lat4[block].astype(F32)

        @pl.loop(0, 16)
        def _(r):
            row = late[pl.ds(r, 1), :]
            full = (jnp.broadcast_to(row, (16, COLS * LAT)) * spread).astype(BF16)
            for g in range(4):
                lhs[r, pl.ds(16 * g, 16)] = full[:, 256 * g : 256 * (g + 1)]

        for i in range(2):
            r = jnp.dot(
                lhs[pl.ds(8 * i, 8)].reshape(8 * COLS, 256), place, preferred_element_type=F32
            )
            t = 2 * block + i
            for y in range(8):
                even, odd = (
                    jnp.concatenate(
                        [r[at : at + 8] for at in range(y * COLS + 8 * par, (y + 1) * COLS, 16)],
                        axis=0,
                    )
                    for par in range(2)
                )
                left, right = before(odd), after(even)
                for ref, base in ((rlo, 0), (rhi, 4)):
                    ref[t + 2, y, 0:HALF] = taps(left, even, odd, base)
                    ref[t + 2, y, HALF:] = taps(even, odd, right, base)

    relayout(half)
    for load in loads2:
        load.wait()
    combine_weights(u2)
    swap.wait_recv()
    relayout(1 - half)

    for load in load_gains + loads0:
        load.wait()

    @pl.loop(0, 4)
    def _(t):
        taps = [(a, b) for a in range(3) for b in range(3)]
        for q in range(5):
            a, b = taps[2 * q]
            v = rlo[t + a, pl.ds(b, TALL)]
            if 2 * q + 1 < 9:
                a, b = taps[2 * q + 1]
                v = v + rhi[t + a, pl.ds(b, TALL)]
            patch[:, 128 * q : 128 * (q + 1)] = v.reshape(TALL * COLS, 128)
        mid[...] = jnp.dot(patch[...], we[...], preferred_element_type=F32)
        for y in range(TALL):
            v = mid[pl.ds(COLS * y, COLS)].astype(BF16)
            if 1 <= y <= ROWS:
                first[t, y - 1] = v
            h = silu_norm(v.astype(F32), 0.5 * g1_ref[...])
            if y == 0:
                h = h * has_up
            if y == TALL - 1:
                h = h * has_down
            put_row(h1, t, y, h[0:HALF], h[HALF:])

    far = lax.rem(band + BANDS - 1 + 2 * odd_band, BANDS)
    near = band + 1 - 2 * odd_band
    far_inside = jnp.where(odd_band == 0, has_up, has_down)
    far_row = 3 * odd_band
    near_row = 3 - far_row
    far_halo = 5 * odd_band
    near_halo = 5 - far_halo
    others = [1 - odd_band + i for i in range(3)]

    def push_to(src, dst, to, send, recv):
        copy = pltpu.make_async_remote_copy(
            src_ref=src,
            dst_ref=dst,
            send_sem=send,
            recv_sem=recv,
            device_id=(seq, to),
            device_id_type=MESH,
        )
        copy.start()
        return copy

    def activate(t, k, y, out=None):
        rows = pl.ds(HALF * k, HALF)
        even = silu_norm(acc[t, 0, rows], 0.5 * g2_ref[...])
        odd = silu_norm(acc[t, 1, rows], 0.5 * g2_ref[...])
        put_row(h2, t, y + 1, even, odd)
        if out is not None:
            out[t, 0:HALF] = even.astype(BF16)
            out[t, HALF:] = odd.astype(BF16)

    conv(h1, u1, acc, [far_row, near_row])
    for t in range(FRAMES):
        activate(t, 0, far_row, slow_out)
    halos = [push_to(slow_out, slow_in, far, hsend.at[0], hrecv.at[0])]
    for t in range(FRAMES):
        activate(t, 1, near_row, fast_out)
    halos.append(push_to(fast_out, fast_in, near, hsend.at[1], hrecv.at[1]))
    conv(h1, u1, acc, [1, 2])
    for t in range(FRAMES):
        activate(t, 0, 1)
        activate(t, 1, 2)

    def finish(t, k, y):
        rows = pl.ds(HALF * k, HALF)
        for par in range(2):
            cols = pl.ds(HALF * par, HALF)
            total = acc[t, par, rows] + first[t, y, cols].astype(F32)
            s_ref[t + 2, y + 1, cols] = total.astype(BF16)

    frames = pl.ds(2, FRAMES)
    halos[1].wait_recv()
    for t in range(FRAMES):
        h = fast_in[t].astype(F32)
        put_row(h2, t, near_halo, h[0:HALF], h[HALF:])
    conv(h2, u2, acc, others)
    for t in range(FRAMES):
        for k in range(3):
            finish(t, k, others[k])
    edges = [
        push_to(
            s_ref.at[frames, near_row + 1],
            s_ref.at[frames, 5 - near_halo],
            near,
            ssend.at[1],
            srecv.at[1],
        )
    ]
    halos[0].wait_recv()
    for t in range(FRAMES):
        h = slow_in[t].astype(F32) * far_inside
        put_row(h2, t, far_halo, h[0:HALF], h[HALF:])
    conv(h2, u2, acc, [far_row])
    for t in range(FRAMES):
        finish(t, 0, far_row)
    edges.append(
        push_to(
            s_ref.at[frames, far_row + 1],
            s_ref.at[frames, 5 - far_halo],
            far,
            ssend.at[0],
            srecv.at[0],
        )
    )

    def double(rows):
        cells = len(rows) * COLS
        stacked = jnp.concatenate(
            [
                jnp.concatenate([s_ref[BLOCK * half + i + a, y] for a in range(3)], axis=1)
                for i in range(BLOCK)
                for y in rows
            ],
            axis=0,
        )
        r = jnp.dot(stacked, wt[...], preferred_element_type=F32)
        for i in range(BLOCK):
            for k, y in enumerate(rows):
                for later in range(2):
                    at = i * cells + k * COLS
                    h = r[at : at + COLS, C * later : C * (later + 1)]
                    even, odd = h[0:HALF], h[HALF:]
                    f = 2 * i + later
                    wide[f, y, :, 0:C] = before(odd).astype(BF16)
                    wide[f, y, :, C : 2 * C] = even.astype(BF16)
                    wide[f, y, :, 2 * C : 3 * C] = odd.astype(BF16)
                    wide[f, y, :, 3 * C : 4 * C] = after(even).astype(BF16)

    def upsample(side, rows):
        py = side + odd_band - 2 * side * odd_band
        at_row = {y: y + odd_band * (3 - 2 * y) for y in rows}
        for px in range(2):
            window = jnp.concatenate(
                [
                    jnp.concatenate(
                        [
                            wide[f, at_row[y] + py + dy, :, C * (px + par) : C * (px + par + 2)]
                            for dy in range(2)
                        ],
                        axis=1,
                    )
                    for f in range(2 * BLOCK)
                    for y in rows
                    for par in range(2)
                ],
                axis=0,
            )
            r = lax.dot_general(
                window,
                phase[2 * py + px],
                (((1,), (1,)), ((), ())),
                preferred_element_type=F32,
            )
            at = 0
            for f in range(2 * BLOCK):
                for y in rows:
                    for par in range(2):
                        cols = pl.ds(2 * par + px, HALF, 4)
                        low[side, f, y, cols, :] = r[at : at + HALF, 0:128]
                        high[side, f, y, cols, :] = r[at : at + HALF, 128:256]
                        at += HALF
        for f in range(2 * BLOCK):
            for y in rows:
                row = 2 * at_row[y] + py
                out_ref[f, row, 0:128] = low[side, f, y].T.astype(BF16)
                out_ref[f, row, 128:CO] = high[side, f, y].T[0 : CO - 128].astype(BF16)

    load_wt.wait()
    edges[0].wait_recv()
    double([1, 2, 3, 4, near_halo])
    upsample(1, [0, 1, 2, 3])
    upsample(0, [1, 2, 3])
    edges[1].wait_recv()
    for t in range(FRAMES):
        s_ref[t + 2, far_halo] = (s_ref[t + 2, far_halo].astype(F32) * far_inside).astype(BF16)
    double([far_halo])
    upsample(0, [0])

    for push in pushes:
        push.wait_send()
    swap.wait_send()
    for copy in halos + edges:
        copy.wait_send()


def decode(lat, arr, we, g1, w1, g2, w2, wt, ws):
    hbm = pl.BlockSpec(memory_space=pltpu.HBM)
    dma = pltpu.SemaphoreType.DMA
    return pl.pallas_call(
        decode_kernel,
        out_shape=jax.ShapeDtypeStruct((2 * BLOCK, 2 * ROWS, CO, 2 * COLS), BF16),
        in_specs=[hbm] * 9,
        out_specs=pl.BlockSpec(memory_space=pltpu.VMEM),
        scratch_shapes=[
            pltpu.SMEM((1, 2 * BANDS), jnp.int32),
            pltpu.VMEM((C,), F32),
            pltpu.VMEM((C,), F32),
            pltpu.VMEM((2 * BANDS, ROWS, COLS * LAT), BF16),
            pltpu.VMEM((2, 16, COLS * LAT), BF16),
            pltpu.VMEM((16, COLS * LAT), F32),
            pltpu.VMEM((16, COLS, 256), BF16),
            pltpu.VMEM((6, 8, COLS, 128), BF16),
            pltpu.VMEM((6, 8, COLS, 128), BF16),
            pltpu.VMEM((TALL * COLS, 640), BF16),
            pltpu.VMEM((TALL * COLS, C), F32),
            pltpu.VMEM((FRAMES, ROWS, COLS, C), BF16),
            pltpu.VMEM((FRAMES, TALL, 4, HALF, C), BF16),
            pltpu.VMEM((FRAMES, TALL, 4, HALF, C), BF16),
            pltpu.VMEM((FRAMES, 2, 3 * HALF, C), F32),
            pltpu.VMEM((FRAMES + 2, TALL, COLS, C), BF16),
            pltpu.VMEM((FRAMES, COLS, C), BF16),
            pltpu.VMEM((FRAMES, COLS, C), BF16),
            pltpu.VMEM((FRAMES, COLS, C), BF16),
            pltpu.VMEM((FRAMES, COLS, C), BF16),
            pltpu.VMEM((640, C), BF16),
            pltpu.VMEM((4, 3, C, 3 * C), BF16),
            pltpu.VMEM((4, 3, C, 3 * C), BF16),
            pltpu.VMEM((3 * C, 2 * C), BF16),
            pltpu.VMEM((9, CO, C), BF16),
            pltpu.VMEM((4, 256, 4 * C), BF16),
            pltpu.VMEM((2 * BLOCK, TALL, HALF, 4 * C), BF16),
            pltpu.VMEM((2, 2 * BLOCK, ROWS, 2 * COLS, 128), F32),
            pltpu.VMEM((2, 2 * BLOCK, ROWS, 2 * COLS, 128), F32),
            dma((33,)),
            dma((BANDS,)),
            dma((BANDS,)),
            dma((2,)),
            dma((2,)),
            dma((2,)),
            dma((2,)),
            dma((2,)),
        ],
        compiler_params=pltpu.CompilerParams(
            collective_id=0, has_side_effects=True, vmem_limit_bytes=50 * 2**20
        ),
        name="decode",
    )(lat, arr, we, g1, w1, g2, w2, wt, ws)


def local(
    transformer_latents,
    tile_arrangement,
    entry_conv_weight,
    first_norm_gain,
    first_conv_weight,
    second_norm_gain,
    second_conv_weight,
    temporal_upscale_weight,
    spatial_upscale_weight,
):
    pin = functools.partial(pltpu.with_memory_space_constraint, memory_space=pltpu.HBM)
    decoded = decode(
        pin(transformer_latents),
        pin(tile_arrangement),
        pin(entry_conv_weight.reshape(27 * LAT, C)),
        pin(first_norm_gain),
        first_conv_weight,
        pin(second_norm_gain),
        second_conv_weight,
        pin(temporal_upscale_weight.reshape(3 * C, 2 * C)),
        pin(jnp.transpose(spatial_upscale_weight, (0, 1, 3, 2)).reshape(9, CO, C)),
    )
    return jnp.transpose(decoded, (0, 1, 3, 2))


def solution(mesh):
    return jax.shard_map(
        local,
        mesh=mesh,
        in_specs=(P("seq", "tile", None), P("seq", None), P(), P(), P(), P(), P(), P(), P()),
        out_specs=P("seq", "tile", None, None),
        check_vma=False,
    )
```

```python
import functools

import jax
import jax.numpy as jnp
from jax import lax
from jax.experimental import pallas as pl
from jax.experimental.pallas import tpu as pltpu
from jax.sharding import PartitionSpec as P

EPS = 1e-06
MESH = pl.DeviceIdType.MESH
F32 = jnp.float32
BF16 = jnp.bfloat16

FRAMES = 4
BLOCK = 2
ROWS = 4
COLS = 64
HALF = COLS // 2
LAT = 16
C = 384
CO = 192
BANDS = 16
TALL = ROWS + 2


def silu_norm(v, gain):
    mean = jnp.sum(v * v, axis=-1, keepdims=True) * (1.0 / C)
    w = v * lax.rsqrt(mean + EPS) * gain
    return w + w * jnp.tanh(w)


def before(odd):
    row = lax.broadcasted_iota(jnp.int32, odd.shape, 0)
    return jnp.where(row == 0, 0.0, pltpu.roll(odd, 1, 0))


def after(even):
    row = lax.broadcasted_iota(jnp.int32, even.shape, 0)
    return jnp.where(row == HALF - 1, 0.0, pltpu.roll(even, HALF - 1, 0))


def put_row(ref, t, y, even, odd):
    ref[t, y, 0] = (before(odd) - odd).astype(BF16)
    ref[t, y, 1] = (even + odd).astype(BF16)
    ref[t, y, 2] = (odd - even).astype(BF16)
    ref[t, y, 3] = (even - after(even)).astype(BF16)


def start_weights(w_hbm, u, sems):
    copies = []
    for a in range(3):
        for e, slot in enumerate((0, 1, 3)):
            copies.append(
                pltpu.make_async_copy(
                    w_hbm.at[a, :, e],
                    u.at[slot, :, :, pl.ds((2 - a) * C, C)],
                    sems.at[3 * a + e],
                )
            )
    return copies


def combine_weights(u):
    @pl.loop(0, 3 * (C // 16))
    def _(i):
        b, r = i // (C // 16), 16 * lax.rem(i, C // 16)
        rows = pl.ds(pl.multiple_of(r, 16), 16)
        outer = u[0, b, rows] + u[3, b, rows]
        inner = u[1, b, rows]
        u[1, b, rows] = (outer + inner) * 0.5
        u[2, b, rows] = (outer - inner) * 0.5


def windows(source, t, frames, k, rows):
    return jnp.concatenate(
        [
            jnp.concatenate([source[t + i, y + b, k] for b in range(3)], axis=1)
            for i in range(frames)
            for y in rows
        ],
        axis=0,
    )


def add(acc, t, k, n, part, fresh):
    if k < 3:
        acc[t, 0, 0:n] = part if fresh and k == 0 else acc[t, 0, 0:n] + part
    if k == 1:
        acc[t, 1, 0:n] = part if fresh else acc[t, 1, 0:n] + part
    elif k > 1:
        acc[t, 1, 0:n] -= part


def conv(source, u, acc, rows, between=None):
    n = HALF * len(rows)
    for k in range(4):
        weight = u[k].reshape(3 * C, 3 * C)
        r = jnp.dot(windows(source, 0, 2, k, rows), weight, preferred_element_type=F32)
        a, b = r[0:n], r[n:]
        add(acc, 0, k, n, a[:, 0:C], True)
        add(acc, 1, k, n, a[:, C : 2 * C] + b[:, 0:C], True)
        add(acc, 2, k, n, a[:, 2 * C :] + b[:, C : 2 * C], True)
        add(acc, 3, k, n, b[:, 2 * C :], True)
    if between is not None:
        between()
    for k in range(4):
        weight = u[k].reshape(3 * C, 3 * C)[:, 0 : 2 * C]
        r = jnp.dot(windows(source, 2, 2, k, rows), weight, preferred_element_type=F32)
        a, b = r[0:n], r[n:]
        add(acc, 2, k, n, a[:, 0:C], False)
        add(acc, 3, k, n, a[:, C:] + b[:, 0:C], False)


def sum_phases(ws, phase):
    spans = (((0,), (1, 2)), ((0, 1), (2,)))
    for py in range(2):
        for px in range(2):
            for dy in range(2):
                for dx in range(2):
                    total = None
                    for ty in spans[py][dy]:
                        for tx in spans[px][dx]:
                            term = ws[3 * ty + tx].astype(F32)
                            total = term if total is None else total + term
                    at = (2 * dy + dx) * C
                    phase[2 * py + px, 0:CO, at : at + C] = total.astype(BF16)
    phase[:, CO:256] = jnp.zeros((4, 256 - CO, 4 * C), BF16)


def decode_kernel(
    lat_hbm,
    arr_hbm,
    we_hbm,
    g1_hbm,
    w1_hbm,
    g2_hbm,
    w2_hbm,
    wt_hbm,
    ws_hbm,
    out_ref,
    arr_ref,
    g1_ref,
    g2_ref,
    gath,
    lat4,
    late,
    lhs,
    rlo,
    rhi,
    patch,
    mid,
    first,
    h1,
    h2,
    acc,
    s_ref,
    slow_out,
    slow_in,
    fast_out,
    fast_in,
    we,
    u1,
    u2,
    wt,
    ws,
    phase,
    wide,
    low,
    high,
    wsem,
    gsend,
    grecv,
    psem,
    hsend,
    hrecv,
    ssend,
    srecv,
):
    seq = lax.axis_index("seq")
    band = lax.axis_index("tile")
    half = lax.rem(seq, 2)
    mate = seq + 1 - 2 * half

    odd_band = lax.rem(band, 2)

    loads1 = start_weights(w1_hbm, u1, wsem.at[pl.ds(0, 9)])
    loads2 = start_weights(w2_hbm, u2, wsem.at[pl.ds(9, 9)])
    loads0 = []
    for p in range(9):
        loads0.append(
            pltpu.make_async_copy(
                we_hbm.at[pl.ds(48 * p, 48)], we.at[pl.ds(64 * p, 48)], wsem.at[18 + p]
            )
        )
    load_wt = pltpu.make_async_copy(wt_hbm, wt, wsem.at[27])
    load_arr = pltpu.make_async_copy(arr_hbm, arr_ref, wsem.at[32])
    load_gains = [
        pltpu.make_async_copy(g1_hbm, g1_ref, wsem.at[30]),
        pltpu.make_async_copy(g2_hbm, g2_ref, wsem.at[31]),
    ]
    load_ws = pltpu.make_async_copy(ws_hbm, ws, wsem.at[28])

    barrier = pltpu.get_barrier_semaphore()
    for d in range(1, BANDS):
        pl.semaphore_signal(
            barrier, inc=1, device_id=(seq, lax.rem(band + d, BANDS)), device_id_type=MESH
        )
    pl.semaphore_signal(barrier, inc=1, device_id=(mate, band), device_id_type=MESH)
    for load in [load_arr] + load_gains + loads1 + loads0 + [load_ws] + loads2 + [load_wt]:
        load.start()
    pl.semaphore_wait(barrier, BANDS)

    pushes = []
    for d in range(1, BANDS):
        pushes.append(
            pltpu.make_async_remote_copy(
                src_ref=lat_hbm,
                dst_ref=gath.at[pl.ds(2 * band, 2)],
                send_sem=gsend.at[d],
                recv_sem=grecv.at[d],
                device_id=(seq, lax.rem(band + d, BANDS)),
                device_id_type=MESH,
            )
        )
    for push in pushes:
        push.start()
    load_own = pltpu.make_async_copy(lat_hbm, gath.at[pl.ds(2 * band, 2)], wsem.at[29])
    load_own.start()
    load_own.wait()

    for p in range(9):
        we[pl.ds(64 * p + 48, 16)] = jnp.zeros((16, C), BF16)
    we[pl.ds(576, 64)] = jnp.zeros((64, C), BF16)
    rlo[0:2] = jnp.zeros((2, 8, COLS, 128), BF16)
    rhi[0:2] = jnp.zeros((2, 8, COLS, 128), BF16)
    s_ref[0:2] = jnp.zeros((2, TALL, COLS, C), BF16)
    load_arr.wait()
    spots = []
    for i in range(BLOCK):
        for o in (-1, 0, 1):
            target = i * BANDS + band + o
            spot = jnp.int32(0)
            for n in range(2 * BANDS):
                spot = jnp.where(arr_ref[0, n] == target, n, spot)
            spots.append(spot)

    for load in loads1:
        load.wait()
    combine_weights(u1)
    load_ws.wait()
    sum_phases(ws, phase)

    for push in pushes:
        push.wait_recv()

    has_up = (band > 0).astype(F32)
    has_down = (band < BANDS - 1).astype(F32)
    picked = []
    for i in range(BLOCK):
        above = gath[spots[3 * i]].astype(F32) * has_up
        own = gath[spots[3 * i + 1]].astype(F32)
        below = gath[spots[3 * i + 2]].astype(F32) * has_down
        picked.append(jnp.concatenate([above[2:4], own, below[0:2]], axis=0))
    lat4[half] = jnp.concatenate(picked, axis=0).astype(BF16)
    swap = pltpu.make_async_remote_copy(
        src_ref=lat4.at[half],
        dst_ref=lat4.at[half],
        send_sem=psem.at[0],
        recv_sem=psem.at[1],
        device_id=(mate, band),
        device_id_type=MESH,
    )
    swap.start()

    place_of = lax.broadcasted_iota(jnp.int32, (16, COLS * LAT), 0)
    column_of = 2 * lax.rem(place_of, 8) + place_of // 8
    spread = (
        lax.rem(lax.broadcasted_iota(jnp.int32, (16, COLS * LAT), 1), 256) // LAT == column_of
    ).astype(F32)
    kk = lax.broadcasted_iota(jnp.int32, (256, 128), 0)
    nn = lax.broadcasted_iota(jnp.int32, (256, 128), 1)
    place = (lax.rem(nn, LAT) == lax.rem(kk, LAT)).astype(F32).astype(BF16)
    lane = lax.broadcasted_iota(jnp.int32, (HALF, 128), 1)
    slot = lane // LAT

    def taps(left, centre, right, base):
        picked = jnp.where(slot == base + 1, centre, 0.0)
        picked = jnp.where(slot == base, left, picked)
        return jnp.where(slot == base + 2, right, picked).astype(BF16)

    def relayout(block):
        late[...] = lat4[block].astype(F32)

        @pl.loop(0, 16)
        def _(r):
            row = late[pl.ds(r, 1), :]
            full = (jnp.broadcast_to(row, (16, COLS * LAT)) * spread).astype(BF16)
            for g in range(4):
                lhs[r, pl.ds(16 * g, 16)] = full[:, 256 * g : 256 * (g + 1)]

        for i in range(2):
            r = jnp.dot(
                lhs[pl.ds(8 * i, 8)].reshape(8 * COLS, 256), place, preferred_element_type=F32
            )
            t = 2 * block + i
            for y in range(8):
                even, odd = (
                    jnp.concatenate(
                        [r[at : at + 8] for at in range(y * COLS + 8 * par, (y + 1) * COLS, 16)],
                        axis=0,
                    )
                    for par in range(2)
                )
                left, right = before(odd), after(even)
                for ref, base in ((rlo, 0), (rhi, 4)):
                    ref[t + 2, y, 0:HALF] = taps(left, even, odd, base)
                    ref[t + 2, y, HALF:] = taps(even, odd, right, base)

    relayout(half)
    for load in loads2:
        load.wait()
    combine_weights(u2)
    swap.wait_recv()
    relayout(1 - half)

    for load in load_gains + loads0:
        load.wait()

    @pl.loop(0, 4)
    def _(t):
        taps = [(a, b) for a in range(3) for b in range(3)]
        for q in range(5):
            a, b = taps[2 * q]
            v = rlo[t + a, pl.ds(b, TALL)]
            if 2 * q + 1 < 9:
                a, b = taps[2 * q + 1]
                v = v + rhi[t + a, pl.ds(b, TALL)]
            patch[:, 128 * q : 128 * (q + 1)] = v.reshape(TALL * COLS, 128)
        mid[...] = jnp.dot(patch[...], we[...], preferred_element_type=F32)
        for y in range(TALL):
            v = mid[pl.ds(COLS * y, COLS)].astype(BF16)
            if 1 <= y <= ROWS:
                first[t, y - 1] = v
            h = silu_norm(v.astype(F32), 0.5 * g1_ref[...])
            if y == 0:
                h = h * has_up
            if y == TALL - 1:
                h = h * has_down
            put_row(h1, t, y, h[0:HALF], h[HALF:])

    far = lax.rem(band + BANDS - 1 + 2 * odd_band, BANDS)
    near = band + 1 - 2 * odd_band
    far_inside = jnp.where(odd_band == 0, has_up, has_down)
    far_row = 3 * odd_band
    near_row = 3 - far_row
    far_halo = 5 * odd_band
    near_halo = 5 - far_halo

    def push_to(src, dst, to, send, recv):
        copy = pltpu.make_async_remote_copy(
            src_ref=src,
            dst_ref=dst,
            send_sem=send,
            recv_sem=recv,
            device_id=(seq, to),
            device_id_type=MESH,
        )
        copy.start()
        return copy

    def activate(t, k, y, out=None):
        rows = pl.ds(HALF * k, HALF)
        even = silu_norm(acc[t, 0, rows], 0.5 * g2_ref[...])
        odd = silu_norm(acc[t, 1, rows], 0.5 * g2_ref[...])
        put_row(h2, t, y + 1, even, odd)
        if out is not None:
            out[t, 0:HALF] = even.astype(BF16)
            out[t, HALF:] = odd.astype(BF16)

    outer = [far_row, near_row]
    far_halos, far_edges = [], []

    def send_hidden(t):
        for i in range(2):
            activate(t + i, 0, far_row, slow_out)
        some = pl.ds(t, 2)
        far_halos.append(
            push_to(slow_out.at[some], slow_in.at[some], far, hsend.at[t], hrecv.at[t])
        )
        for i in range(2):
            activate(t + i, 1, near_row, fast_out)

    conv(h1, u1, acc, outer, lambda: send_hidden(0))
    send_hidden(2)
    near_halos = push_to(fast_out, fast_in, near, hsend.at[1], hrecv.at[1])
    conv(h1, u1, acc, [1, 2])
    for t in range(FRAMES):
        activate(t, 0, 1)
        activate(t, 1, 2)

    def finish(t, k, y):
        rows = pl.ds(HALF * k, HALF)
        for par in range(2):
            cols = pl.ds(HALF * par, HALF)
            total = acc[t, par, rows] + first[t, y, cols].astype(F32)
            s_ref[t + 2, y + 1, cols] = total.astype(BF16)

    def take_far(t):
        far_halos[t // 2].wait_recv()
        for i in range(2):
            h = slow_in[t + i].astype(F32) * far_inside
            put_row(h2, t + i, far_halo, h[0:HALF], h[HALF:])

    def send_second(t):
        for i in range(2):
            finish(t + i, 0, far_row)
        some = pl.ds(t + 2, 2)
        far_edges.append(
            push_to(
                s_ref.at[some, far_row + 1],
                s_ref.at[some, 5 - far_halo],
                far,
                ssend.at[t],
                srecv.at[t],
            )
        )
        for i in range(2):
            finish(t + i, 1, near_row)

    conv(h2, u2, acc, [1, 2])
    for t in range(FRAMES):
        finish(t, 0, 1)
        finish(t, 1, 2)
    near_halos.wait_recv()
    for t in range(FRAMES):
        h = fast_in[t].astype(F32)
        put_row(h2, t, near_halo, h[0:HALF], h[HALF:])
    take_far(0)

    def middle():
        send_second(0)
        take_far(2)

    conv(h2, u2, acc, outer, middle)
    send_second(2)
    frames = pl.ds(2, FRAMES)
    near_edges = push_to(
        s_ref.at[frames, near_row + 1],
        s_ref.at[frames, 5 - near_halo],
        near,
        ssend.at[1],
        srecv.at[1],
    )

    def double(rows):
        cells = len(rows) * COLS
        stacked = jnp.concatenate(
            [
                jnp.concatenate([s_ref[BLOCK * half + i + a, y] for a in range(3)], axis=1)
                for i in range(BLOCK)
                for y in rows
            ],
            axis=0,
        )
        r = jnp.dot(stacked, wt[...], preferred_element_type=F32)
        for i in range(BLOCK):
            for k, y in enumerate(rows):
                for later in range(2):
                    at = i * cells + k * COLS
                    h = r[at : at + COLS, C * later : C * (later + 1)]
                    even, odd = h[0:HALF], h[HALF:]
                    f = 2 * i + later
                    wide[f, y, :, 0:C] = before(odd).astype(BF16)
                    wide[f, y, :, C : 2 * C] = even.astype(BF16)
                    wide[f, y, :, 2 * C : 3 * C] = odd.astype(BF16)
                    wide[f, y, :, 3 * C : 4 * C] = after(even).astype(BF16)

    def upsample(side, rows):
        py = side + odd_band - 2 * side * odd_band
        at_row = {y: y + odd_band * (3 - 2 * y) for y in rows}
        for px in range(2):
            window = jnp.concatenate(
                [
                    jnp.concatenate(
                        [
                            wide[f, at_row[y] + py + dy, :, C * (px + par) : C * (px + par + 2)]
                            for dy in range(2)
                        ],
                        axis=1,
                    )
                    for f in range(2 * BLOCK)
                    for y in rows
                    for par in range(2)
                ],
                axis=0,
            )
            r = lax.dot_general(
                window,
                phase[2 * py + px],
                (((1,), (1,)), ((), ())),
                preferred_element_type=F32,
            )
            at = 0
            for f in range(2 * BLOCK):
                for y in rows:
                    for par in range(2):
                        cols = pl.ds(2 * par + px, HALF, 4)
                        low[side, f, y, cols, :] = r[at : at + HALF, 0:128]
                        high[side, f, y, cols, :] = r[at : at + HALF, 128:256]
                        at += HALF
        for f in range(2 * BLOCK):
            for y in rows:
                row = 2 * at_row[y] + py
                out_ref[f, row, 0:128] = low[side, f, y].T.astype(BF16)
                out_ref[f, row, 128:CO] = high[side, f, y].T[0 : CO - 128].astype(BF16)

    load_wt.wait()
    double([1, 2, 3, 4])
    near_edges.wait_recv()
    double([near_halo])
    upsample(1, [0, 1, 2, 3])
    upsample(0, [1, 2, 3])
    for copy in far_edges:
        copy.wait_recv()
    for t in range(FRAMES):
        s_ref[t + 2, far_halo] = (s_ref[t + 2, far_halo].astype(F32) * far_inside).astype(BF16)
    double([far_halo])
    upsample(0, [0])

    for push in pushes:
        push.wait_send()
    swap.wait_send()
    for copy in far_halos + far_edges + [near_halos, near_edges]:
        copy.wait_send()


def decode(lat, arr, we, g1, w1, g2, w2, wt, ws):
    hbm = pl.BlockSpec(memory_space=pltpu.HBM)
    dma = pltpu.SemaphoreType.DMA
    return pl.pallas_call(
        decode_kernel,
        out_shape=jax.ShapeDtypeStruct((2 * BLOCK, 2 * ROWS, CO, 2 * COLS), BF16),
        in_specs=[hbm] * 9,
        out_specs=pl.BlockSpec(memory_space=pltpu.VMEM),
        scratch_shapes=[
            pltpu.SMEM((1, 2 * BANDS), jnp.int32),
            pltpu.VMEM((C,), F32),
            pltpu.VMEM((C,), F32),
            pltpu.VMEM((2 * BANDS, ROWS, COLS * LAT), BF16),
            pltpu.VMEM((2, 16, COLS * LAT), BF16),
            pltpu.VMEM((16, COLS * LAT), F32),
            pltpu.VMEM((16, COLS, 256), BF16),
            pltpu.VMEM((6, 8, COLS, 128), BF16),
            pltpu.VMEM((6, 8, COLS, 128), BF16),
            pltpu.VMEM((TALL * COLS, 640), BF16),
            pltpu.VMEM((TALL * COLS, C), F32),
            pltpu.VMEM((FRAMES, ROWS, COLS, C), BF16),
            pltpu.VMEM((FRAMES, TALL, 4, HALF, C), BF16),
            pltpu.VMEM((FRAMES, TALL, 4, HALF, C), BF16),
            pltpu.VMEM((FRAMES, 2, 3 * HALF, C), F32),
            pltpu.VMEM((FRAMES + 2, TALL, COLS, C), BF16),
            pltpu.VMEM((FRAMES, COLS, C), BF16),
            pltpu.VMEM((FRAMES, COLS, C), BF16),
            pltpu.VMEM((FRAMES, COLS, C), BF16),
            pltpu.VMEM((FRAMES, COLS, C), BF16),
            pltpu.VMEM((640, C), BF16),
            pltpu.VMEM((4, 3, C, 3 * C), BF16),
            pltpu.VMEM((4, 3, C, 3 * C), BF16),
            pltpu.VMEM((3 * C, 2 * C), BF16),
            pltpu.VMEM((9, CO, C), BF16),
            pltpu.VMEM((4, 256, 4 * C), BF16),
            pltpu.VMEM((2 * BLOCK, TALL, HALF, 4 * C), BF16),
            pltpu.VMEM((2, 2 * BLOCK, ROWS, 2 * COLS, 128), F32),
            pltpu.VMEM((2, 2 * BLOCK, ROWS, 2 * COLS, 128), F32),
            dma((33,)),
            dma((BANDS,)),
            dma((BANDS,)),
            dma((2,)),
            dma((3,)),
            dma((3,)),
            dma((3,)),
            dma((3,)),
        ],
        compiler_params=pltpu.CompilerParams(
            collective_id=0, has_side_effects=True, vmem_limit_bytes=50 * 2**20
        ),
        name="decode",
    )(lat, arr, we, g1, w1, g2, w2, wt, ws)


def local(
    transformer_latents,
    tile_arrangement,
    entry_conv_weight,
    first_norm_gain,
    first_conv_weight,
    second_norm_gain,
    second_conv_weight,
    temporal_upscale_weight,
    spatial_upscale_weight,
):
    pin = functools.partial(pltpu.with_memory_space_constraint, memory_space=pltpu.HBM)
    decoded = decode(
        pin(transformer_latents),
        pin(tile_arrangement),
        pin(entry_conv_weight.reshape(27 * LAT, C)),
        pin(first_norm_gain),
        first_conv_weight,
        pin(second_norm_gain),
        second_conv_weight,
        pin(temporal_upscale_weight.reshape(3 * C, 2 * C)),
        pin(jnp.transpose(spatial_upscale_weight, (0, 1, 3, 2)).reshape(9, CO, C)),
    )
    return jnp.transpose(decoded, (0, 1, 3, 2))


def solution(mesh):
    return jax.shard_map(
        local,
        mesh=mesh,
        in_specs=(P("seq", "tile", None), P("seq", None), P(), P(), P(), P(), P(), P(), P()),
        out_specs=P("seq", "tile", None, None),
        check_vma=False,
    )
```

```python
import functools

import jax
import jax.numpy as jnp
from jax import lax
from jax.experimental import pallas as pl
from jax.experimental.pallas import tpu as pltpu
from jax.sharding import PartitionSpec as P

EPS = 1e-06
MESH = pl.DeviceIdType.MESH
F32 = jnp.float32
BF16 = jnp.bfloat16

FRAMES = 4
BLOCK = 2
ROWS = 4
COLS = 64
HALF = COLS // 2
LAT = 16
C = 384
CO = 192
BANDS = 16
TALL = ROWS + 2


def silu_norm(v, gain):
    mean = jnp.sum(v * v, axis=-1, keepdims=True) * (1.0 / C)
    w = v * lax.rsqrt(mean + EPS) * gain
    return w + w * jnp.tanh(w)


def before(odd):
    row = lax.broadcasted_iota(jnp.int32, odd.shape, 0)
    return jnp.where(row == 0, 0.0, pltpu.roll(odd, 1, 0))


def after(even):
    row = lax.broadcasted_iota(jnp.int32, even.shape, 0)
    return jnp.where(row == HALF - 1, 0.0, pltpu.roll(even, HALF - 1, 0))


def put_row(ref, t, y, even, odd):
    ref[t, y, 0] = (before(odd) - odd).astype(BF16)
    ref[t, y, 1] = (even + odd).astype(BF16)
    ref[t, y, 2] = (odd - even).astype(BF16)
    ref[t, y, 3] = (even - after(even)).astype(BF16)


def start_weights(w_hbm, u, sems):
    copies = []
    for a in range(3):
        for e, slot in enumerate((0, 1, 3)):
            copies.append(
                pltpu.make_async_copy(
                    w_hbm.at[a, :, e],
                    u.at[slot, :, :, pl.ds((2 - a) * C, C)],
                    sems.at[3 * a + e],
                )
            )
    return copies


def combine_weights(u):
    @pl.loop(0, 3 * (C // 16))
    def _(i):
        b, r = i // (C // 16), 16 * lax.rem(i, C // 16)
        rows = pl.ds(pl.multiple_of(r, 16), 16)
        outer = u[0, b, rows] + u[3, b, rows]
        inner = u[1, b, rows]
        u[1, b, rows] = (outer + inner) * 0.5
        u[2, b, rows] = (outer - inner) * 0.5


def windows(source, t, frames, k, rows):
    return jnp.concatenate(
        [
            jnp.concatenate([source[t + i, y + b, k] for b in range(3)], axis=1)
            for i in range(frames)
            for y in rows
        ],
        axis=0,
    )


def add(acc, t, k, n, part, fresh):
    if k < 3:
        acc[t, 0, 0:n] = part if fresh and k == 0 else acc[t, 0, 0:n] + part
    if k == 1:
        acc[t, 1, 0:n] = part if fresh else acc[t, 1, 0:n] + part
    elif k > 1:
        acc[t, 1, 0:n] -= part


def conv(source, u, acc, rows, between=None):
    n = HALF * len(rows)
    for k in range(4):
        weight = u[k].reshape(3 * C, 3 * C)
        r = jnp.dot(windows(source, 0, 2, k, rows), weight, preferred_element_type=F32)
        a, b = r[0:n], r[n:]
        add(acc, 0, k, n, a[:, 0:C], True)
        add(acc, 1, k, n, a[:, C : 2 * C] + b[:, 0:C], True)
        add(acc, 2, k, n, a[:, 2 * C :] + b[:, C : 2 * C], True)
        add(acc, 3, k, n, b[:, 2 * C :], True)
    if between is not None:
        between()
    for k in range(4):
        weight = u[k].reshape(3 * C, 3 * C)[:, 0 : 2 * C]
        r = jnp.dot(windows(source, 2, 2, k, rows), weight, preferred_element_type=F32)
        a, b = r[0:n], r[n:]
        add(acc, 2, k, n, a[:, 0:C], False)
        add(acc, 3, k, n, a[:, C:] + b[:, 0:C], False)


def sum_phases(ws, phase):
    spans = (((0,), (1, 2)), ((0, 1), (2,)))
    for py in range(2):
        for px in range(2):
            for dy in range(2):
                for dx in range(2):
                    total = None
                    for ty in spans[py][dy]:
                        for tx in spans[px][dx]:
                            term = ws[3 * ty + tx].astype(F32)
                            total = term if total is None else total + term
                    at = (2 * dy + dx) * C
                    phase[2 * py + px, 0:CO, at : at + C] = total.astype(BF16)
    phase[:, CO:256] = jnp.zeros((4, 256 - CO, 4 * C), BF16)


def decode_kernel(
    lat_hbm,
    arr_hbm,
    we_hbm,
    g1_hbm,
    w1_hbm,
    g2_hbm,
    w2_hbm,
    wt_hbm,
    ws_hbm,
    out_ref,
    arr_ref,
    g1_ref,
    g2_ref,
    gath,
    lat4,
    late,
    lhs,
    rlo,
    rhi,
    first,
    h1,
    h2,
    acc,
    s_ref,
    slow_out,
    slow_in,
    fast_out,
    fast_in,
    we,
    u1,
    u2,
    wt,
    ws,
    phase,
    wide,
    low,
    high,
    wsem,
    gsend,
    grecv,
    psem,
    hsend,
    hrecv,
    ssend,
    srecv,
):
    seq = lax.axis_index("seq")
    band = lax.axis_index("tile")
    half = lax.rem(seq, 2)
    mate = seq + 1 - 2 * half

    odd_band = lax.rem(band, 2)

    loads1 = start_weights(w1_hbm, u1, wsem.at[pl.ds(0, 9)])
    loads2 = start_weights(w2_hbm, u2, wsem.at[pl.ds(9, 9)])
    loads0 = []
    for p in range(9):
        loads0.append(
            pltpu.make_async_copy(
                we_hbm.at[pl.ds(48 * p, 48)], we.at[pl.ds(64 * p, 48)], wsem.at[18 + p]
            )
        )
    load_wt = pltpu.make_async_copy(wt_hbm, wt, wsem.at[27])
    load_arr = pltpu.make_async_copy(arr_hbm, arr_ref, wsem.at[32])
    load_gains = [
        pltpu.make_async_copy(g1_hbm, g1_ref, wsem.at[30]),
        pltpu.make_async_copy(g2_hbm, g2_ref, wsem.at[31]),
    ]
    load_ws = pltpu.make_async_copy(ws_hbm, ws, wsem.at[28])

    barrier = pltpu.get_barrier_semaphore()
    for d in range(1, BANDS):
        pl.semaphore_signal(
            barrier, inc=1, device_id=(seq, lax.rem(band + d, BANDS)), device_id_type=MESH
        )
    pl.semaphore_signal(barrier, inc=1, device_id=(mate, band), device_id_type=MESH)
    for load in [load_arr] + load_gains + loads1 + loads0 + [load_ws] + loads2 + [load_wt]:
        load.start()
    pl.semaphore_wait(barrier, BANDS)

    pushes = []
    for d in range(1, BANDS):
        pushes.append(
            pltpu.make_async_remote_copy(
                src_ref=lat_hbm,
                dst_ref=gath.at[pl.ds(2 * band, 2)],
                send_sem=gsend.at[d],
                recv_sem=grecv.at[d],
                device_id=(seq, lax.rem(band + d, BANDS)),
                device_id_type=MESH,
            )
        )
    for push in pushes:
        push.start()
    load_own = pltpu.make_async_copy(lat_hbm, gath.at[pl.ds(2 * band, 2)], wsem.at[29])
    load_own.start()
    load_own.wait()

    for p in range(9):
        we[pl.ds(64 * p + 48, 16)] = jnp.zeros((16, C), BF16)
    we[pl.ds(576, 64)] = jnp.zeros((64, C), BF16)
    rlo[0:2] = jnp.zeros((2, 8, COLS, 128), BF16)
    rhi[0:2] = jnp.zeros((2, 8, COLS, 128), BF16)
    s_ref[0:2] = jnp.zeros((2, TALL, COLS, C), BF16)
    load_arr.wait()
    spots = []
    for i in range(BLOCK):
        for o in (-1, 0, 1):
            target = i * BANDS + band + o
            spot = jnp.int32(0)
            for n in range(2 * BANDS):
                spot = jnp.where(arr_ref[0, n] == target, n, spot)
            spots.append(spot)

    for load in loads1:
        load.wait()
    combine_weights(u1)
    load_ws.wait()
    sum_phases(ws, phase)

    for push in pushes:
        push.wait_recv()

    has_up = (band > 0).astype(F32)
    has_down = (band < BANDS - 1).astype(F32)
    picked = []
    for i in range(BLOCK):
        above = gath[spots[3 * i]].astype(F32) * has_up
        own = gath[spots[3 * i + 1]].astype(F32)
        below = gath[spots[3 * i + 2]].astype(F32) * has_down
        picked.append(jnp.concatenate([above[2:4], own, below[0:2]], axis=0))
    lat4[half] = jnp.concatenate(picked, axis=0).astype(BF16)
    swap = pltpu.make_async_remote_copy(
        src_ref=lat4.at[half],
        dst_ref=lat4.at[half],
        send_sem=psem.at[0],
        recv_sem=psem.at[1],
        device_id=(mate, band),
        device_id_type=MESH,
    )
    swap.start()

    place_of = lax.broadcasted_iota(jnp.int32, (16, COLS * LAT), 0)
    column_of = 2 * lax.rem(place_of, 8) + place_of // 8
    spread = (
        lax.rem(lax.broadcasted_iota(jnp.int32, (16, COLS * LAT), 1), 256) // LAT == column_of
    ).astype(F32)
    kk = lax.broadcasted_iota(jnp.int32, (256, 128), 0)
    nn = lax.broadcasted_iota(jnp.int32, (256, 128), 1)
    place = (lax.rem(nn, LAT) == lax.rem(kk, LAT)).astype(F32).astype(BF16)
    lane = lax.broadcasted_iota(jnp.int32, (HALF, 128), 1)
    slot = lane // LAT

    def taps(left, centre, right, base):
        picked = jnp.where(slot == base + 1, centre, 0.0)
        picked = jnp.where(slot == base, left, picked)
        return jnp.where(slot == base + 2, right, picked).astype(BF16)

    def relayout(block):
        late[...] = lat4[block].astype(F32)

        @pl.loop(0, 16)
        def _(r):
            row = late[pl.ds(r, 1), :]
            full = (jnp.broadcast_to(row, (16, COLS * LAT)) * spread).astype(BF16)
            for g in range(4):
                lhs[r, pl.ds(16 * g, 16)] = full[:, 256 * g : 256 * (g + 1)]

        for i in range(2):
            r = jnp.dot(
                lhs[pl.ds(8 * i, 8)].reshape(8 * COLS, 256), place, preferred_element_type=F32
            )
            t = 2 * block + i
            for y in range(8):
                even, odd = (
                    jnp.concatenate(
                        [r[at : at + 8] for at in range(y * COLS + 8 * par, (y + 1) * COLS, 16)],
                        axis=0,
                    )
                    for par in range(2)
                )
                left, right = before(odd), after(even)
                for ref, base in ((rlo, 0), (rhi, 4)):
                    ref[t + 2, y, 0:HALF] = taps(left, even, odd, base)
                    ref[t + 2, y, HALF:] = taps(even, odd, right, base)

    relayout(half)
    for load in loads2:
        load.wait()
    combine_weights(u2)
    swap.wait_recv()
    relayout(1 - half)

    for load in load_gains + loads0:
        load.wait()

    spans = [(a, b) for a in range(3) for b in range(3)]
    for t in range(FRAMES):
        parts = []
        for q in range(5):
            a, b = spans[2 * q]
            v = rlo[t + a, b : b + TALL]
            if 2 * q + 1 < 9:
                a, b = spans[2 * q + 1]
                v = v + rhi[t + a, b : b + TALL]
            parts.append(v.reshape(TALL * COLS, 128))
        entry = jnp.dot(
            jnp.concatenate(parts, axis=1), we[...], preferred_element_type=F32
        ).astype(BF16)
        for y in range(TALL):
            v = entry[COLS * y : COLS * (y + 1)]
            if 1 <= y <= ROWS:
                first[t, y - 1] = v
            h = silu_norm(v.astype(F32), 0.5 * g1_ref[...])
            if y == 0:
                h = h * has_up
            if y == TALL - 1:
                h = h * has_down
            put_row(h1, t, y, h[0:HALF], h[HALF:])

    far = lax.rem(band + BANDS - 1 + 2 * odd_band, BANDS)
    near = band + 1 - 2 * odd_band
    far_inside = jnp.where(odd_band == 0, has_up, has_down)
    far_row = 3 * odd_band
    near_row = 3 - far_row
    far_halo = 5 * odd_band
    near_halo = 5 - far_halo

    def push_to(src, dst, to, send, recv):
        copy = pltpu.make_async_remote_copy(
            src_ref=src,
            dst_ref=dst,
            send_sem=send,
            recv_sem=recv,
            device_id=(seq, to),
            device_id_type=MESH,
        )
        copy.start()
        return copy

    def activate(t, k, y, out=None):
        rows = pl.ds(HALF * k, HALF)
        even = silu_norm(acc[t, 0, rows], 0.5 * g2_ref[...])
        odd = silu_norm(acc[t, 1, rows], 0.5 * g2_ref[...])
        put_row(h2, t, y + 1, even, odd)
        if out is not None:
            out[t, 0:HALF] = even.astype(BF16)
            out[t, HALF:] = odd.astype(BF16)

    outer = [far_row, near_row]
    far_halos, far_edges = [], []

    def send_hidden(t):
        for i in range(2):
            activate(t + i, 0, far_row, slow_out)
        some = pl.ds(t, 2)
        far_halos.append(
            push_to(slow_out.at[some], slow_in.at[some], far, hsend.at[t], hrecv.at[t])
        )
        for i in range(2):
            activate(t + i, 1, near_row, fast_out)

    conv(h1, u1, acc, outer, lambda: send_hidden(0))
    send_hidden(2)
    near_halos = push_to(fast_out, fast_in, near, hsend.at[1], hrecv.at[1])
    conv(h1, u1, acc, [1, 2])
    for t in range(FRAMES):
        activate(t, 0, 1)
        activate(t, 1, 2)

    def finish(t, k, y):
        rows = pl.ds(HALF * k, HALF)
        for par in range(2):
            cols = pl.ds(HALF * par, HALF)
            total = acc[t, par, rows] + first[t, y, cols].astype(F32)
            s_ref[t + 2, y + 1, cols] = total.astype(BF16)

    def take_far(t):
        far_halos[t // 2].wait_recv()
        for i in range(2):
            h = slow_in[t + i].astype(F32) * far_inside
            put_row(h2, t + i, far_halo, h[0:HALF], h[HALF:])

    def send_second(t):
        for i in range(2):
            finish(t + i, 0, far_row)
        some = pl.ds(t + 2, 2)
        far_edges.append(
            push_to(
                s_ref.at[some, far_row + 1],
                s_ref.at[some, 5 - far_halo],
                far,
                ssend.at[t],
                srecv.at[t],
            )
        )
        for i in range(2):
            finish(t + i, 1, near_row)

    conv(h2, u2, acc, [1, 2])
    for t in range(FRAMES):
        finish(t, 0, 1)
        finish(t, 1, 2)
    near_halos.wait_recv()
    for t in range(FRAMES):
        h = fast_in[t].astype(F32)
        put_row(h2, t, near_halo, h[0:HALF], h[HALF:])
    take_far(0)

    def middle():
        send_second(0)
        take_far(2)

    conv(h2, u2, acc, outer, middle)
    send_second(2)
    frames = pl.ds(2, FRAMES)
    near_edges = push_to(
        s_ref.at[frames, near_row + 1],
        s_ref.at[frames, 5 - near_halo],
        near,
        ssend.at[1],
        srecv.at[1],
    )

    def double(rows):
        cells = len(rows) * COLS
        stacked = jnp.concatenate(
            [
                jnp.concatenate([s_ref[BLOCK * half + i + a, y] for a in range(3)], axis=1)
                for i in range(BLOCK)
                for y in rows
            ],
            axis=0,
        )
        r = jnp.dot(stacked, wt[...], preferred_element_type=F32)
        for i in range(BLOCK):
            for k, y in enumerate(rows):
                for later in range(2):
                    at = i * cells + k * COLS
                    h = r[at : at + COLS, C * later : C * (later + 1)]
                    even, odd = h[0:HALF], h[HALF:]
                    f = 2 * i + later
                    wide[f, y, :, 0:C] = before(odd).astype(BF16)
                    wide[f, y, :, C : 2 * C] = even.astype(BF16)
                    wide[f, y, :, 2 * C : 3 * C] = odd.astype(BF16)
                    wide[f, y, :, 3 * C : 4 * C] = after(even).astype(BF16)

    def upsample(side, rows):
        py = side + odd_band - 2 * side * odd_band
        at_row = {y: y + odd_band * (3 - 2 * y) for y in rows}
        for px in range(2):
            window = jnp.concatenate(
                [
                    jnp.concatenate(
                        [
                            wide[f, at_row[y] + py + dy, :, C * (px + par) : C * (px + par + 2)]
                            for dy in range(2)
                        ],
                        axis=1,
                    )
                    for f in range(2 * BLOCK)
                    for y in rows
                    for par in range(2)
                ],
                axis=0,
            )
            r = lax.dot_general(
                window,
                phase[2 * py + px],
                (((1,), (1,)), ((), ())),
                preferred_element_type=F32,
            )
            at = 0
            for f in range(2 * BLOCK):
                for y in rows:
                    for par in range(2):
                        cols = pl.ds(2 * par + px, HALF, 4)
                        low[side, f, y, cols, :] = r[at : at + HALF, 0:128]
                        high[side, f, y, cols, :] = r[at : at + HALF, 128:256]
                        at += HALF
        for f in range(2 * BLOCK):
            for y in rows:
                row = 2 * at_row[y] + py
                out_ref[f, row, 0:128] = low[side, f, y].T.astype(BF16)
                out_ref[f, row, 128:CO] = high[side, f, y].T[0 : CO - 128].astype(BF16)

    load_wt.wait()
    double([1, 2, 3, 4])
    near_edges.wait_recv()
    double([near_halo])
    upsample(1, [0, 1, 2, 3])
    upsample(0, [1, 2, 3])
    for copy in far_edges:
        copy.wait_recv()
    for t in range(FRAMES):
        s_ref[t + 2, far_halo] = (s_ref[t + 2, far_halo].astype(F32) * far_inside).astype(BF16)
    double([far_halo])
    upsample(0, [0])

    for push in pushes:
        push.wait_send()
    swap.wait_send()
    for copy in far_halos + far_edges + [near_halos, near_edges]:
        copy.wait_send()


def decode(lat, arr, we, g1, w1, g2, w2, wt, ws):
    hbm = pl.BlockSpec(memory_space=pltpu.HBM)
    dma = pltpu.SemaphoreType.DMA
    return pl.pallas_call(
        decode_kernel,
        out_shape=jax.ShapeDtypeStruct((2 * BLOCK, 2 * ROWS, CO, 2 * COLS), BF16),
        in_specs=[hbm] * 9,
        out_specs=pl.BlockSpec(memory_space=pltpu.VMEM),
        scratch_shapes=[
            pltpu.SMEM((1, 2 * BANDS), jnp.int32),
            pltpu.VMEM((C,), F32),
            pltpu.VMEM((C,), F32),
            pltpu.VMEM((2 * BANDS, ROWS, COLS * LAT), BF16),
            pltpu.VMEM((2, 16, COLS * LAT), BF16),
            pltpu.VMEM((16, COLS * LAT), F32),
            pltpu.VMEM((16, COLS, 256), BF16),
            pltpu.VMEM((6, 8, COLS, 128), BF16),
            pltpu.VMEM((6, 8, COLS, 128), BF16),
            pltpu.VMEM((FRAMES, ROWS, COLS, C), BF16),
            pltpu.VMEM((FRAMES, TALL, 4, HALF, C), BF16),
            pltpu.VMEM((FRAMES, TALL, 4, HALF, C), BF16),
            pltpu.VMEM((FRAMES, 2, 3 * HALF, C), F32),
            pltpu.VMEM((FRAMES + 2, TALL, COLS, C), BF16),
            pltpu.VMEM((FRAMES, COLS, C), BF16),
            pltpu.VMEM((FRAMES, COLS, C), BF16),
            pltpu.VMEM((FRAMES, COLS, C), BF16),
            pltpu.VMEM((FRAMES, COLS, C), BF16),
            pltpu.VMEM((640, C), BF16),
            pltpu.VMEM((4, 3, C, 3 * C), BF16),
            pltpu.VMEM((4, 3, C, 3 * C), BF16),
            pltpu.VMEM((3 * C, 2 * C), BF16),
            pltpu.VMEM((9, CO, C), BF16),
            pltpu.VMEM((4, 256, 4 * C), BF16),
            pltpu.VMEM((2 * BLOCK, TALL, HALF, 4 * C), BF16),
            pltpu.VMEM((2, 2 * BLOCK, ROWS, 2 * COLS, 128), F32),
            pltpu.VMEM((2, 2 * BLOCK, ROWS, 2 * COLS, 128), F32),
            dma((33,)),
            dma((BANDS,)),
            dma((BANDS,)),
            dma((2,)),
            dma((3,)),
            dma((3,)),
            dma((3,)),
            dma((3,)),
        ],
        compiler_params=pltpu.CompilerParams(
            collective_id=0, has_side_effects=True, vmem_limit_bytes=50 * 2**20
        ),
        name="decode",
    )(lat, arr, we, g1, w1, g2, w2, wt, ws)


def local(
    transformer_latents,
    tile_arrangement,
    entry_conv_weight,
    first_norm_gain,
    first_conv_weight,
    second_norm_gain,
    second_conv_weight,
    temporal_upscale_weight,
    spatial_upscale_weight,
):
    pin = functools.partial(pltpu.with_memory_space_constraint, memory_space=pltpu.HBM)
    decoded = decode(
        pin(transformer_latents),
        pin(tile_arrangement),
        pin(entry_conv_weight.reshape(27 * LAT, C)),
        pin(first_norm_gain),
        first_conv_weight,
        pin(second_norm_gain),
        second_conv_weight,
        pin(temporal_upscale_weight.reshape(3 * C, 2 * C)),
        pin(jnp.transpose(spatial_upscale_weight, (0, 1, 3, 2)).reshape(9, CO, C)),
    )
    return jnp.transpose(decoded, (0, 1, 3, 2))


def solution(mesh):
    return jax.shard_map(
        local,
        mesh=mesh,
        in_specs=(P("seq", "tile", None), P("seq", None), P(), P(), P(), P(), P(), P(), P()),
        out_specs=P("seq", "tile", None, None),
        check_vma=False,
    )
```
